768 devices in a mesh: gx: 16 (over y, core), gy: 48 (over x, z).
Axes of the slice: x: 4, y: 8, z: 12, core: 2. Of those that a mesh axis runs over, the one named last changes fastest.
Arguments:
- atm_state: float32 [8, 1024, 6144], P(None, 'gx', 'gy'), may hold values from -6 to 6
- ocean_temp: float32 [10, 2048, 6144], P(None, 'gx', 'gy'), may hold values from -6 to 6
- flux_coef: float32 [12, 8], replicated, may hold values from -2 to 2
- flux_mix: float32 [10, 12], replicated, may hold values from -1.75 to 1.75
- intersect_share: bfloat16 [16, 4608, 128, 128], P('gx', 'gy'), may hold values from -0.5 to 0.5
- sender_tile_line: int32 [16, 4608], P('gx', 'gy'), may hold values from 0 to 63
- dest_tile_line: int32 [16, 4608], P('gx', 'gy'), may hold values from 0 to 127
- dst_owner: int32 [16, 4608, 1], P('gx', 'gy'), may hold values from 0 to 47; in each aligned block of 96 rows (0 to 95, 96 to 191, ..., all dimensions but the last counted through in order) at most 4 rows name the same one
Outputs:
- marine_final_heat: float32 [10, 2048, 6144], P(None, 'gx', 'gy')
- aerial_water_heat: float32 [1024, 6144], P('gx', 'gy')
The draws below stay inside these ranges and needn't reach their ends.
Inputs may be any that keep to these rules, and one draw needn't show every extreme that they name: `dst_owner`: among the 96 blocks q with the same g and the same q // 96, no owner is named more than 4 times, a bound that some block reaches.
All inputs are finite; a program needn't handle non-finite values.
Results may differ from the reference program's by a relative error of at most 0.003.
Values may be sent and summed in bfloat16 or wider, within the bound.
A program may use at most 32 MiB of HBM per device.

```python
import math
import jax
import jax.numpy as jnp
import numpy as np
from jax import lax

AXD = 64
AYD = 128
MARINE_TILE_LINES = 128
MARINE_LINE_SPAN = 128
LEV_A = 8
LEV_O = 10
FLUXES = 12
NB = 96
CAP = 4
AIR_LINE_COUNT = 1024
AIR_LINE_SPAN = 6144
OX = 2048
OY = 6144
QROW = 4608
N_GX = 16
N_GY = 48


def set_ends(drawn, rng, least, top_value):
    index_at = [jax.random.randint(jax.random.fold_in(rng, axis), (), 0, length) for axis, length in enumerate(drawn.shape)]
    longest = drawn.shape.index(max(drawn.shape))
    neighbour = index_at[:longest] + [(index_at[longest] + 1) % drawn.shape[longest]] + index_at[longest + 1:]
    return drawn.at[tuple(index_at)].set(least).at[tuple(neighbour)].set(top_value)


def steps_of(stream_key, extent, cuts, least, largest):
    def one(dim, blocks):
        steps = jax.random.uniform(jax.random.fold_in(jax.random.fold_in(stream_key, 6), dim), (blocks,), jnp.float32, least / len(cuts), largest / len(cuts))
        return jnp.repeat(jnp.exp(steps), extent[dim] // blocks).reshape((-1,) + (1,) * (len(extent) - dim - 1))

    level = one(*cuts[0])
    for cut in cuts[1:]:
        level = level * one(*cut)
    return level


def shared_out(stream_key, own, number, rows, number_of, top, bound, skew):
    ranking = jax.random.permutation(stream_key, number_of)
    heavy_load, usual = shares(number_of, rows * top, bound, skew, True), shares(number_of, rows * top, bound, skew, False)
    places = jnp.arange(number_of)

    def named(lengths, rotation):
        used = int((lengths > 0).sum())
        fixed = max(1, used // 4)
        moved = fixed + (places - fixed + rotation * (used - fixed)) % max(1, number_of - fixed)
        return jnp.zeros((number_of,), jnp.int32).at[ranking[jnp.where(places < fixed, places, moved)]].set(jnp.asarray(lengths, jnp.int32))

    lengths = jnp.where(number % 4 == 0, named(heavy_load, number // 4), named(usual, number - number // 4 - 1))
    mixed = jax.random.permutation(jax.random.fold_in(own, 3), number_of)
    donor, taker = mixed[0:number_of // 2 * 2:2], mixed[1:number_of // 2 * 2:2]
    margin = jnp.minimum(lengths[donor] - 1, bound - lengths[taker]) // 2
    margin = jnp.where((donor == ranking[0]) | (taker == ranking[0]) | (lengths[taker] == 0), 0, jnp.maximum(margin, 0))
    moved = jax.random.randint(jax.random.fold_in(own, 4), (number_of // 2,), 0, 1 << 20) % (margin + 1)
    lengths = lengths.at[donor].add(-moved).at[taker].add(moved)
    labels = jnp.searchsorted(jnp.cumsum(lengths), jnp.arange(rows * top), side="right").astype(jnp.int32)
    table = labels.reshape(top, rows).T
    table = table[jax.random.permutation(jax.random.fold_in(own, 1), rows)]
    rotation = jax.random.randint(jax.random.fold_in(own, 2), (rows, 1), 0, top)
    return jnp.take_along_axis(table, (jnp.arange(top)[None, :] + rotation) % top, axis=1)


def shares(number_of, total, limit, lean, full):
    portions = [(1 << 20) // math.isqrt(rank ** lean) + 1 for rank in range(1, number_of + 1)]
    largest = limit if full else min(limit, max(-(-total // number_of), total * portions[0] // sum(portions)))
    least = 1 if total - largest >= number_of - 1 else 0
    given, surplus = [largest] + [least] * (number_of - 1), total - largest - least * (number_of - 1)
    while surplus > 0:
        candidates = [i for i in range(1, number_of) if given[i] < largest] or [i for i in range(1, number_of) if given[i] < limit]
        mass, remaining = sum([portions[i] for i in candidates]), surplus
        for i in candidates:
            addition = min(limit - given[i], max(1, remaining * portions[i] // mass), surplus)
            given[i] = given[i] + addition
            surplus = surplus - addition
    return np.array(given)


def bell_draw(rng, extent, scale, most, split=(), kind=jnp.bfloat16):
    factor_of = steps_of(rng, extent, split, -0.22, 0.18) if split else 1.0
    entries = jax.random.normal(rng, extent, jnp.float32) * scale * factor_of
    return jnp.minimum(jnp.maximum(entries, -most), most).astype(kind)


def setup_inputs(seed: int = 0) -> dict:
    streams_of = jax.random.split(jax.random.key(seed), 9)
    atm_state = bell_draw(streams_of[0], (LEV_A, AIR_LINE_COUNT, AIR_LINE_SPAN), 1.0, 6.0, ((1, 16), (2, 48)), jnp.float32)
    ocean_temp = bell_draw(streams_of[1], (LEV_O, OX, OY), 1.0, 6.0, ((1, 16), (2, 48)), jnp.float32)
    flux_coef = bell_draw(streams_of[2], (FLUXES, LEV_A), LEV_A ** -0.5, 2.0, (), jnp.float32)
    flux_mix = bell_draw(streams_of[3], (LEV_O, FLUXES), FLUXES ** -0.5, 1.75, (), jnp.float32)
    intersect_share = bell_draw(streams_of[4], (N_GX, QROW, AYD, MARINE_LINE_SPAN), AYD ** -0.5, 0.5, ((0, 16), (1, 48)))
    sender_tile_line = set_ends(jax.random.randint(streams_of[5], (N_GX, QROW), 0, AXD), jax.random.fold_in(streams_of[5], 1), 0, AXD - 1).astype(jnp.int32)
    dest_tile_line = set_ends(jax.random.randint(streams_of[6], (N_GX, QROW), 0, MARINE_TILE_LINES), jax.random.fold_in(streams_of[6], 1), 0, MARINE_TILE_LINES - 1).astype(jnp.int32)
    dst_owner_keys = jax.random.split(jax.random.fold_in(streams_of[7], 1), N_GX * QROW // NB)
    dst_owner_turns = jax.random.permutation(jax.random.fold_in(streams_of[7], 3), N_GX * QROW // NB)
    dst_owner = jax.vmap(lambda own, number: shared_out(jax.random.fold_in(streams_of[7], 2), own, number, NB, N_GY, 1, CAP, 2))(dst_owner_keys, dst_owner_turns).reshape((N_GX, QROW, 1))
    return {"atm_state": atm_state, "ocean_temp": ocean_temp, "flux_coef": flux_coef, "flux_mix": flux_mix, "intersect_share": intersect_share, "sender_tile_line": sender_tile_line, "dest_tile_line": dest_tile_line, "dst_owner": dst_owner}


diffusion_rate = 0.2
forcing_step = 0.5


def spread_laterally(field):
    padded = jnp.pad(field, ((0, 0), (1, 1), (1, 1)))
    beside_all = padded[:, :-2, 1:-1] + padded[:, 2:, 1:-1] + padded[:, 1:-1, :-2] + padded[:, 1:-1, 2:]
    return field + diffusion_rate * (beside_all - 4.0 * field)


def reference(atm_state, ocean_temp, flux_coef, flux_mix, intersect_share, sender_tile_line, dest_tile_line, dst_owner):
    atm_mid = spread_laterally(atm_state)
    atm_surface = spread_laterally(atm_mid)
    fluxes = jnp.tanh(jnp.einsum("kl,lxy->kxy", flux_coef, atm_surface, precision=lax.Precision.HIGHEST)).astype(jnp.bfloat16)
    flux_grid = fluxes.reshape(FLUXES, N_GX, AXD, N_GY, AYD)
    column_block = jnp.arange(N_GY * NB, dtype=jnp.int32) // NB
    line_ordinal_series = jnp.arange(N_GX, dtype=jnp.int32)
    keeper_tiles = dst_owner[:, :, 0]

    def forward_row(items):
        line_place_slot, share_grid_array, src_row, dest_line, keeper_line = items
        flux_row = lax.dynamic_index_in_dim(flux_grid, line_place_slot, 1, keepdims=False)
        tile_rows = flux_row[:, src_row, column_block, :]
        contrib = jnp.einsum("kqi,qio->qko", tile_rows.astype(jnp.float32), share_grid_array.astype(jnp.float32), precision=lax.Precision.HIGHEST)
        landed = jnp.zeros((MARINE_TILE_LINES, N_GY, FLUXES, MARINE_LINE_SPAN), jnp.float32)
        return landed.at[dest_line, keeper_line].add(contrib)

    ocean_flux = lax.map(forward_row, (line_ordinal_series, intersect_share, sender_tile_line, dest_tile_line, keeper_tiles))
    forcing = jnp.einsum("lk,gxhky->lgxhy", flux_mix, ocean_flux, precision=lax.Precision.HIGHEST).reshape(LEV_O, OX, OY)
    marine_initial_state = ocean_temp + forcing_step * forcing
    marine_middle_state = spread_laterally(marine_initial_state)
    marine_final_heat = spread_laterally(marine_middle_state)
    skin_heat_field = marine_final_heat[0].astype(jnp.bfloat16).reshape(N_GX, MARINE_TILE_LINES, N_GY, MARINE_LINE_SPAN)

    def homebound_line(items):
        line_place_slot, share_grid_array, src_row, dest_line, keeper_line = items
        skin_heat_line = lax.dynamic_index_in_dim(skin_heat_field, line_place_slot, 0, keepdims=False)
        chosen_lines = skin_heat_line[dest_line, keeper_line]
        value_entries = jnp.einsum("awq,aq->aw", share_grid_array.astype(jnp.float32), chosen_lines.astype(jnp.float32), precision=lax.Precision.HIGHEST)
        landed = jnp.zeros((AXD, N_GY, AYD), jnp.float32)
        return landed.at[src_row, column_block].add(value_entries)

    aerial_water_heat = lax.map(homebound_line, (line_ordinal_series, intersect_share, sender_tile_line, dest_tile_line, keeper_tiles)).reshape(AIR_LINE_COUNT, AIR_LINE_SPAN)
    return marine_final_heat, aerial_water_heat
```

```python
import functools

import jax
import jax.numpy as jnp
from jax import lax
from jax.experimental import pallas as pl
from jax.experimental.pallas import tpu as pltpu
from jax.sharding import PartitionSpec as P

MESH = pl.DeviceIdType.MESH
RATE = 0.2
CAP = 4
F32, BF16, I32 = jnp.float32, jnp.bfloat16, jnp.int32
LANES = 128
NT = (((1,), (1,)), ((), ()))
CHUNK = 16


def iota(shape, dim):
    return lax.broadcasted_iota(I32, shape, dim)


def pack_sides(levels, rows):
    pair = lax.shift_right_logical(iota((rows, LANES), 1), 1)
    packed = jnp.zeros((rows, LANES), F32)
    for n, field in enumerate(levels):
        packed = jnp.where(pair == n, pltpu.roll(field, 2 * n, 1) if n else field, packed)
        packed = jnp.where(pair == 32 + n, pltpu.roll(field, 66 + 2 * n, 1), packed)
    return packed


class Halo:
    def __init__(self, place, refs, rows, count):
        self.gx, self.gy, self.ngx, self.ngy = place
        (self.top, self.bot, self.cl, self.cr, self.dg, self.ptl, self.ptr, self.pe, self.pk, self.ss, self.rs) = refs
        self.rows, self.count = rows, count

    def start(self, field, packed):
        rows = self.rows
        tall = packed
        if rows < LANES:
            tall = jnp.concatenate([packed, jnp.zeros((LANES - rows, LANES), F32)], axis=0)
        turned = tall.T
        cs = self.ptl.shape[0]
        self.ptl[...] = turned[0:cs]
        self.ptr[...] = turned[64 : 64 + cs]
        self.pe[0] = packed[0:8]
        self.pe[1] = packed[rows - 8 : rows]
        self.pk[...] = packed
        up, down = lax.rem(self.gx + self.ngx - 1, self.ngx), lax.rem(self.gx + 1, self.ngx)
        left, right = lax.rem(self.gy + self.ngy - 1, self.ngy), lax.rem(self.gy + 1, self.ngy)
        plan = (
            (field.at[:, 0:8], self.bot, (up, self.gy)),
            (field.at[:, rows - 8 : rows], self.top, (down, self.gy)),
            (self.ptl, self.cr, (self.gx, left)),
            (self.ptr, self.cl, (self.gx, right)),
            (self.pe.at[0], self.dg.at[3], (up, left)),
            (self.pe.at[0], self.dg.at[2], (up, right)),
            (self.pe.at[1], self.dg.at[1], (down, left)),
            (self.pe.at[1], self.dg.at[0], (down, right)),
        )
        self.copies = [
            pltpu.make_async_remote_copy(
                src_ref=src,
                dst_ref=dst,
                send_sem=self.ss.at[n],
                recv_sem=self.rs.at[n],
                device_id=device,
                device_id_type=MESH,
            )
            for n, (src, dst, device) in enumerate(plan)
        ]
        for copy in self.copies:
            copy.start()

    def arrive(self):
        for copy in self.copies:
            copy.wait_recv()
        rows = self.rows
        lane = iota((1, LANES), 1)
        low = lane < 64
        self.has_top, self.has_bot = self.gx > 0, self.gx < self.ngx - 1
        edge = jnp.where(low, jnp.where(self.gy > 0, 1, 0), jnp.where(self.gy < self.ngy - 1, 1, 0)) > 0
        cs = self.cl.shape[0]
        fill = jnp.zeros((64 - cs, LANES), F32)
        turned = jnp.concatenate([self.cl[...], fill, self.cr[...], fill], axis=0)
        sides = turned.T[0:rows]
        above = jnp.where(low, pltpu.roll(self.dg[0], 64, 1), pltpu.roll(self.dg[1], 64, 1))
        below = jnp.where(low, pltpu.roll(self.dg[2], 64, 1), pltpu.roll(self.dg[3], 64, 1))
        above = jnp.where(self.has_top, above, 0.0)
        below = jnp.where(self.has_bot, below, 0.0)
        rim = jnp.where(edge, jnp.concatenate([above, sides, below], axis=0), 0.0)
        total = rows + 16
        up = pltpu.roll(rim, 1, 0)[8 : rows + 8]
        down = pltpu.roll(rim, total - 1, 0)[8 : rows + 8]
        near = sides + self.pk[...]
        beside = jnp.where(low, pltpu.roll(near, 1, 1), pltpu.roll(near, LANES - 1, 1))
        mid = sides + RATE * (up + down + beside - 4.0 * sides)
        self.rim, self.mid = rim, jnp.where(edge, mid, 0.0)

    def two_steps(self, n, field, rim_ref, mid_ref):
        rows = self.rows
        total = rows + 16
        rim, rim_mid = rim_ref[...], mid_ref[...]
        top = jnp.where(self.has_top, self.top[n], 0.0)
        bot = jnp.where(self.has_bot, self.bot[n], 0.0)
        whole = jnp.concatenate([top, field, bot], axis=0)
        lane, row = iota((total, LANES), 1), iota((total, LANES), 0)
        to_first, to_last = LANES - 1 - 2 * n, 63 - 2 * n
        beside = (
            jnp.where(lane == 0, pltpu.roll(rim, to_first, 1), pltpu.roll(whole, 1, 1))
            + jnp.where(lane == LANES - 1, pltpu.roll(rim, to_last, 1), pltpu.roll(whole, LANES - 1, 1))
            + pltpu.roll(whole, 1, 0)
            + pltpu.roll(whole, total - 1, 0)
        )
        mid = whole + RATE * (beside - 4.0 * whole)
        first_row, last_row = jnp.where(self.has_top, 0, 8), jnp.where(self.has_bot, total, rows + 8)
        mid = jnp.where((row >= first_row) & (row < last_row), mid, 0.0)
        own = mid[8 : rows + 8]
        lane = iota((rows, LANES), 1)
        beside = (
            jnp.where(lane == 0, pltpu.roll(rim_mid, to_first, 1), pltpu.roll(own, 1, 1))
            + jnp.where(lane == LANES - 1, pltpu.roll(rim_mid, to_last, 1), pltpu.roll(own, LANES - 1, 1))
            + pltpu.roll(mid, 1, 0)[8 : rows + 8]
            + pltpu.roll(mid, total - 1, 0)[8 : rows + 8]
        )
        return own + RATE * (beside - 4.0 * own)

    def wait_sent(self):
        for copy in self.copies:
            copy.wait_send()


def kernel(
    sizes,
    atm_ref,
    ocean_hbm,
    coef_ref,
    mix_ref,
    share_hbm,
    src_ref,
    dest_ref,
    owner_ref,
    final_hbm,
    aerial_ref,
    share,
    ocean,
    final,
    surf,
    mixed,
    lists,
    table,
    table_s,
    id_send,
    id_recv,
    f_send,
    f_recv,
    hits,
    spread,
    pick,
    s_send,
    s_recv,
    rims,
    mids,
    share_sem,
    ocean_sem,
    table_sem,
    final_sem,
    id_ss,
    id_rs,
    f_ss,
    f_rs,
    s_ss,
    s_rs,
    *halo_refs,
):
    ngx, nx, nz = sizes
    ngy = nx * nz
    slots = ngy * CAP
    chunks = ngy // CHUNK
    la, ra = atm_ref.shape[0], atm_ref.shape[1]
    lo, ro = ocean.shape[0], ocean.shape[1]
    nb = src_ref.shape[1]
    fluxes = coef_ref.shape[0]
    gx, gy = lax.axis_index("gx"), lax.axis_index("gy")
    my_x, my_z = lax.div(gy, nz), lax.rem(gy, nz)
    place = (gx, gy, ngx, ngy)

    share_copy = pltpu.make_async_copy(share_hbm.at[0], share, share_sem)
    share_copy.start()
    ocean_copy = pltpu.make_async_copy(ocean_hbm, ocean, ocean_sem)
    ocean_copy.start()

    def shift(i):
        k = lax.div(i, nx)
        dx = lax.rem(i, nx)
        dz = lax.div(k + 1, 2) * (2 * lax.rem(k, 2) - 1)
        return dx, dz

    def ahead(i):
        dx, dz = shift(i)
        return lax.rem(my_x + dx, nx) * nz + lax.rem(my_z + dz + nz, nz)

    def behind(i):
        dx, dz = shift(i)
        return lax.rem(my_x - dx + nx, nx) * nz + lax.rem(my_z - dz + nz, nz)

    barrier = pltpu.get_barrier_semaphore()
    up, down = lax.rem(gx + ngx - 1, ngx), lax.rem(gx + 1, ngx)
    left, right = lax.rem(gy + ngy - 1, ngy), lax.rem(gy + 1, ngy)
    for device in ((up, gy), (down, gy), (up, left), (up, right), (down, left), (down, right)):
        pl.semaphore_signal(barrier, inc=1, device_id=device, device_id_type=MESH)

    def greet(i, carry):
        pl.semaphore_signal(barrier, inc=1, device_id=(gx, ahead(i)), device_id_type=MESH)
        return carry

    lax.fori_loop(1, ngy, greet, 0)

    atm_halo = Halo(place, halo_refs[0:11], ra, la)
    top_halo = Halo(place, halo_refs[11:22], ro, 1)
    low_halo = Halo(place, halo_refs[22:33], ro, lo - 1)

    lists[...] = jnp.full((8, LANES), -1, I32)
    lists[0:1, 0:nb] = owner_ref[...]
    lists[1:2, 0:nb] = dest_ref[...]
    own_row, dest_row = lists[0:1, :], lists[1:2, :]
    lane = iota((1, LANES), 1)
    own_x = jnp.zeros((1, LANES), I32)
    for t in range(1, nx):
        own_x = own_x + jnp.where(own_row >= t * nz, 1, 0)
    own_z = own_row - own_x * nz
    dx = own_x - my_x
    dx = jnp.where(dx < 0, dx + nx, dx)
    dz = own_z - my_z
    dz = jnp.where(dz < 0, dz + nz, dz)
    k = jnp.where(dz == 0, 0, jnp.where(dz <= nz // 2, 2 * dz - 1, 2 * (nz - dz)))
    step_row = k * nx + dx
    sq = (LANES, LANES)
    sub_q, lane_q = iota(sq, 0), iota(sq, 1)
    own_sq = jnp.broadcast_to(own_row, sq)
    same = (own_sq == own_sq.T) & (sub_q < lane_q)
    rank = jnp.sum(jnp.where(same, 1, 0), axis=0, keepdims=True)
    slot_row = jnp.where(lane < nb, step_row * CAP + rank, -1)
    slot_col = jnp.broadcast_to(slot_row, sq).T
    table[...] = jnp.zeros((8, LANES), I32)
    table[0:1, :] = jnp.clip(slot_row, 0, slots - 1)
    for b in range(-(-slots // LANES)):
        hit = slot_col == lane_q + b * LANES
        block = jnp.sum(jnp.where(hit, sub_q, 0), axis=0, keepdims=True)
        table[1 + b : 2 + b, :] = jnp.clip(block, 0, nb - 1)
    table_copy = pltpu.make_async_copy(table, table_s, table_sem)
    table_copy.start()
    wide = (ngy, LANES)
    step_i, lane_i = iota(wide, 0), iota(wide, 1)
    slot_w = jnp.broadcast_to(slot_row, wide)
    line_w = jnp.broadcast_to((dest_row + 1).astype(F32), wide)
    ids = jnp.zeros(wide, F32)
    for j in range(CAP):
        line = jnp.sum(jnp.where(slot_w == step_i * CAP + j, line_w, 0.0), axis=1, keepdims=True)
        ids = jnp.where(lax.rem(lane_i, CAP) == j, jnp.broadcast_to(line, wide), ids)
    ids = jnp.where(lax.div(lane_i, 16) == lax.rem(step_i, 8), ids, 0.0)
    id_send[...] = ids.reshape(ngy, 1, LANES)
    id_recv[0] = id_send[0]

    atm_packed = pack_sides([atm_ref[l] for l in range(la)], ra)

    pl.semaphore_wait(barrier, ngy - 1 + 6)

    atm_halo.start(atm_ref, atm_packed)

    def id_copy(i):
        return pltpu.make_async_remote_copy(
            src_ref=id_send.at[i],
            dst_ref=id_recv.at[i],
            send_sem=id_ss,
            recv_sem=id_rs,
            device_id=(gx, ahead(i)),
            device_id_type=MESH,
        )

    def send_ids(i, carry):
        id_copy(i).start()
        return carry

    lax.fori_loop(1, ngy, send_ids, 0)

    atm_halo.arrive()
    rims[0, 0 : ra + 16] = atm_halo.rim
    mids[0, 0:ra] = atm_halo.mid

    def atm_level(l, carry):
        surf[l] = atm_halo.two_steps(l, atm_ref[l], rims.at[0, 0 : ra + 16], mids.at[0, 0:ra])
        return carry

    lax.fori_loop(0, la, atm_level, 0)

    band = 16

    def flux_band(c, carry):
        r0 = pl.multiple_of(c * band, band)
        fields = [surf[l, pl.ds(r0, band)] for l in range(la)]
        flux = []
        for kk in range(fluxes):
            total = coef_ref[kk, 0] * fields[0]
            for l in range(1, la):
                total = total + coef_ref[kk, l] * fields[l]
            flux.append(jnp.tanh(total).astype(BF16).astype(F32))
        for l in range(lo):
            total = mix_ref[l, 0] * flux[0]
            for kk in range(1, fluxes):
                total = total + mix_ref[l, kk] * flux[kk]
            total = 0.5 * total
            for j in range(CAP):
                mixed[pl.ds(pl.multiple_of((l * CAP + j) * ra + r0, band), band)] = total
        return carry

    lax.fori_loop(0, ra // band, flux_band, 0)

    share_copy.wait()
    table_copy.wait()

    f_rows = f_send.shape[1]
    used = lo * CAP
    slot_of_row = lax.rem(iota((used, LANES), 0), CAP)

    def f_copy(i):
        return pltpu.make_async_remote_copy(
            src_ref=f_send.at[i],
            dst_ref=f_recv.at[i],
            send_sem=f_ss,
            recv_sem=f_rs.at[lax.div(i, CHUNK)],
            device_id=(gx, ahead(i)),
            device_id_type=MESH,
        )

    def contribution(i):
        left_parts, right_parts = [], []
        for j in range(CAP):
            s = i * CAP + j
            q = jnp.clip(table_s[1 + lax.div(s, LANES), lax.rem(s, LANES)], 0, nb - 1)
            rows = mixed[pl.ds(src_ref[0, q], used, stride=ra), :]
            rows = jnp.where(slot_of_row == j, rows, 0.0)
            rows = jnp.concatenate([rows, jnp.zeros((f_rows - used, LANES), F32)], axis=0)
            left_parts.append(rows.astype(BF16))
            right_parts.append(share[q])
        return jnp.dot(
            jnp.concatenate(left_parts, axis=1),
            jnp.concatenate(right_parts, axis=0),
            preferred_element_type=F32,
        ).astype(BF16)

    def send_blocks(t, carry):
        i = ngy - 1 - t
        f_send[i] = contribution(i)
        f_copy(i).start()
        return carry

    lax.fori_loop(0, ngy - 1, send_blocks, 0)
    f_recv[0] = contribution(0)

    pltpu.make_async_remote_copy(
        src_ref=id_send.at[1:ngy],
        dst_ref=id_recv.at[1:ngy],
        send_sem=id_ss,
        recv_sem=id_rs,
        device_id=(gx, gy),
        device_id_type=MESH,
    ).wait_recv()
    line_of_row = iota((ro, LANES), 0) + 1
    level_of_lane = lax.rem(lax.div(iota((ro, LANES), 1), CAP), CAP)
    for g in range(ngy // 8):
        ids_row = id_recv[8 * g]
        for t in range(1, 8):
            ids_row = ids_row + id_recv[8 * g + t]
        hit = jnp.where(jnp.broadcast_to(ids_row.astype(I32), (ro, LANES)) == line_of_row, 1.0, 0.0)
        hits[:, g * LANES : (g + 1) * LANES] = hit.astype(BF16)
        half = (g % 2) * LANES
        for l in range(CAP):
            spread[g // 2, l * ro : (l + 1) * ro, half : half + LANES] = jnp.where(
                level_of_lane == l, hit, 0.0
            ).astype(BF16)
    chosen = iota((slots, ngy * 16), 0)
    chosen = jnp.where(
        iota((slots, ngy * 16), 1) == lax.div(chosen, CAP) * 16 + lax.rem(chosen, CAP), 1.0, 0.0
    ).astype(BF16)
    pick[...] = lax.dot_general(chosen, hits[...], NT, preferred_element_type=F32).astype(BF16)

    ocean_copy.wait()

    def land(c, l0, l1):
        base = 4 * (l0 // 4)
        rows = f_recv[c * CHUNK : (c + 1) * CHUNK, base * CAP : base * CAP + 16, :]
        landed = jnp.dot(
            spread[c, (l0 - base) * ro : (l1 - base) * ro, :],
            rows.reshape(CHUNK * 16, LANES),
            preferred_element_type=F32,
        )
        for l in range(l0, l1):
            ocean[l] = ocean[l] + landed[(l - l0) * ro : (l - l0 + 1) * ro]

    for c in reversed(range(chunks)):
        first = 1 if c == 0 else c * CHUNK
        here = pl.ds(first, (c + 1) * CHUNK - first)
        pltpu.make_async_remote_copy(
            src_ref=f_send.at[here],
            dst_ref=f_recv.at[here],
            send_sem=f_ss,
            recv_sem=f_rs.at[c],
            device_id=(gx, gy),
            device_id_type=MESH,
        ).wait_recv()
        if c:
            for l0 in range(0, lo, 4):
                land(c, l0, min(lo, l0 + 4))
    land(0, 0, 1)
    top_halo.start(ocean.at[0:1], pack_sides([ocean[0]], ro))
    land(0, 1, 4)
    for l0 in range(4, lo, 4):
        land(0, l0, min(lo, l0 + 4))
    low_halo.start(ocean.at[1:lo], pack_sides([ocean[l] for l in range(1, lo)], ro))

    top_halo.arrive()
    rims[1] = top_halo.rim
    mids[1] = top_halo.mid
    skin = top_halo.two_steps(0, ocean[0], rims.at[1], mids.at[1])
    final[0] = skin
    lines = jnp.dot(pick[...], skin.astype(BF16), preferred_element_type=F32)
    s_send[...] = lines.reshape(slots, 1, LANES)
    s_recv[0:CAP] = s_send[0:CAP]

    def s_copy(i):
        here = pl.ds(i * CAP, CAP)
        return pltpu.make_async_remote_copy(
            src_ref=s_send.at[here],
            dst_ref=s_recv.at[here],
            send_sem=s_ss,
            recv_sem=s_rs,
            device_id=(gx, behind(i)),
            device_id_type=MESH,
        )

    def send_lines(t, carry):
        s_copy(ngy - 1 - t).start()
        return carry

    lax.fori_loop(0, ngy - 1, send_lines, 0)

    low_halo.arrive()
    rims[2] = low_halo.rim
    mids[2] = low_halo.mid

    def low_level(n, carry):
        final[n + 1] = low_halo.two_steps(n, ocean[n + 1], rims.at[2], mids.at[2])
        return carry

    lax.fori_loop(0, lo - 1, low_level, 0)
    final_copy = pltpu.make_async_copy(final, final_hbm, final_sem)
    final_copy.start()

    rest = pl.ds(CAP, slots - CAP)
    pltpu.make_async_remote_copy(
        src_ref=s_send.at[rest],
        dst_ref=s_recv.at[rest],
        send_sem=s_ss,
        recv_sem=s_rs,
        device_id=(gx, gy),
        device_id_type=MESH,
    ).wait_recv()
    row_a = iota((ra, LANES), 0)

    def home(b, total):
        left_parts, right_parts = [], []
        for j in range(4):
            q = b * 4 + j
            line = jnp.broadcast_to(s_recv[jnp.clip(table_s[0, q], 0, slots - 1)], (ra, LANES))
            left_parts.append(jnp.where(row_a == src_ref[0, q], line, 0.0).astype(BF16))
            right_parts.append(share[q])
        return total + lax.dot_general(
            jnp.concatenate(left_parts, axis=1),
            jnp.concatenate(right_parts, axis=1),
            NT,
            preferred_element_type=F32,
        )

    aerial_ref[...] = lax.fori_loop(0, nb // 4, home, jnp.zeros((ra, LANES), F32))

    for halo in (atm_halo, top_halo, low_halo):
        halo.wait_sent()
    for buffer, sem, first in ((id_send, id_ss, 1), (f_send, f_ss, 1), (s_send, s_ss, CAP)):
        here = pl.ds(first, buffer.shape[0] - first)
        pltpu.make_async_remote_copy(
            src_ref=buffer.at[here],
            dst_ref=buffer.at[here],
            send_sem=sem,
            recv_sem=s_rs,
            device_id=(gx, gy),
            device_id_type=MESH,
        ).wait_send()
    final_copy.wait()


def halo_scratch(rows, count):
    cs = -(-2 * count // 8) * 8
    return [
        pltpu.VMEM((count, 8, LANES), F32),
        pltpu.VMEM((count, 8, LANES), F32),
        pltpu.VMEM((cs, LANES), F32),
        pltpu.VMEM((cs, LANES), F32),
        pltpu.VMEM((4, 8, LANES), F32),
        pltpu.VMEM((cs, LANES), F32),
        pltpu.VMEM((cs, LANES), F32),
        pltpu.VMEM((2, 8, LANES), F32),
        pltpu.VMEM((rows, LANES), F32),
        pltpu.SemaphoreType.DMA((8,)),
        pltpu.SemaphoreType.DMA((8,)),
    ]


def body(sizes, atm_state, ocean_temp, flux_coef, flux_mix, share, src, dest, owner):
    ngx, nx, nz = sizes
    ngy = nx * nz
    slots = ngy * CAP
    la, ra, _ = atm_state.shape
    lo, ro, _ = ocean_temp.shape
    nb = src.shape[1]
    f_rows = -(-lo * CAP // 16) * 16
    vmem = pl.BlockSpec(memory_space=pltpu.VMEM)
    smem = pl.BlockSpec(memory_space=pltpu.SMEM)
    anywhere = pl.BlockSpec(memory_space=pl.ANY)
    dma = pltpu.SemaphoreType.DMA
    return pl.pallas_call(
        functools.partial(kernel, sizes),
        out_shape=(
            jax.ShapeDtypeStruct(ocean_temp.shape, F32),
            jax.ShapeDtypeStruct((ra, LANES), F32),
        ),
        in_specs=[vmem, anywhere, smem, smem, anywhere, smem, vmem, vmem],
        out_specs=(anywhere, vmem),
        scratch_shapes=[
            pltpu.VMEM((nb, LANES, LANES), BF16),
            pltpu.VMEM((lo, ro, LANES), F32),
            pltpu.VMEM((lo, ro, LANES), F32),
            pltpu.VMEM((la, ra, LANES), F32),
            pltpu.VMEM((lo * CAP * ra, LANES), F32),
            pltpu.VMEM((8, LANES), I32),
            pltpu.VMEM((8, LANES), I32),
            pltpu.SMEM((8, LANES), I32),
            pltpu.VMEM((ngy, 1, LANES), F32),
            pltpu.VMEM((ngy, 1, LANES), F32),
            pltpu.VMEM((ngy, f_rows, LANES), BF16),
            pltpu.VMEM((ngy, f_rows, LANES), BF16),
            pltpu.VMEM((ro, ngy * 16), BF16),
            pltpu.VMEM((ngy // CHUNK, 4 * ro, CHUNK * 16), BF16),
            pltpu.VMEM((slots, ro), BF16),
            pltpu.VMEM((slots, 1, LANES), F32),
            pltpu.VMEM((slots, 1, LANES), F32),
            pltpu.VMEM((3, ro + 16, LANES), F32),
            pltpu.VMEM((3, ro, LANES), F32),
            dma,
            dma,
            dma,
            dma,
            dma,
            dma,
            dma,
            dma((ngy // CHUNK,)),
            dma,
            dma,
            *halo_scratch(ra, la),
            *halo_scratch(ro, 1),
            *halo_scratch(ro, lo - 1),
        ],
        compiler_params=pltpu.CompilerParams(
            collective_id=0, has_side_effects=True, vmem_limit_bytes=48 * 1024 * 1024
        ),
        cost_estimate=pl.CostEstimate(flops=200_000_000, bytes_accessed=5_000_000, transcendentals=100_000),
    )(atm_state, ocean_temp, flux_coef, flux_mix, share, src, dest, owner.reshape(1, nb))


def solution(mesh):
    ngy = mesh.shape["gy"]
    nx = 4
    return jax.shard_map(
        functools.partial(body, (mesh.shape["gx"], nx, ngy // nx)),
        mesh=mesh,
        in_specs=(
            P(None, "gx", "gy"),
            P(None, "gx", "gy"),
            P(),
            P(),
            P("gx", "gy", None, None),
            P("gx", "gy"),
            P("gx", "gy"),
            P("gx", "gy", None),
        ),
        out_specs=(P(None, "gx", "gy"), P("gx", "gy")),
        check_vma=False,
    )
```

```python
import functools

import jax
import jax.numpy as jnp
from jax import lax
from jax.experimental import pallas as pl
from jax.experimental.pallas import tpu as pltpu
from jax.sharding import PartitionSpec as P

MESH = pl.DeviceIdType.MESH
RATE = 0.2
CAP = 4
F32, BF16, I32 = jnp.float32, jnp.bfloat16, jnp.int32
LANES = 128
NT = (((1,), (1,)), ((), ()))
GROUP = 2
SPAN = GROUP * CAP
CHUNK = LANES // SPAN
UNROLL = 4
BURST = 8


def iota(shape, dim):
    return lax.broadcasted_iota(I32, shape, dim)


def pack_sides(levels, rows):
    pair = lax.shift_right_logical(iota((rows, LANES), 1), 1)
    packed = jnp.zeros((rows, LANES), F32)
    for n, field in enumerate(levels):
        packed = jnp.where(pair == n, pltpu.roll(field, 2 * n, 1) if n else field, packed)
        packed = jnp.where(pair == 32 + n, pltpu.roll(field, 66 + 2 * n, 1), packed)
    return packed


class Halo:
    def __init__(self, place, refs, rows, count):
        self.gx, self.gy, self.ngx, self.ngy = place
        (self.top, self.bot, self.cl, self.cr, self.dg, self.ptl, self.ptr, self.pe, self.pk, self.ss, self.rs) = refs
        self.rows, self.count = rows, count

    def start(self, field, levels):
        rows = self.rows
        up, down = lax.rem(self.gx + self.ngx - 1, self.ngx), lax.rem(self.gx + 1, self.ngx)
        left, right = lax.rem(self.gy + self.ngy - 1, self.ngy), lax.rem(self.gy + 1, self.ngy)
        plan = (
            (field.at[:, 0:8], self.bot, (up, self.gy)),
            (field.at[:, rows - 8 : rows], self.top, (down, self.gy)),
            (self.ptl, self.cr, (self.gx, left)),
            (self.ptr, self.cl, (self.gx, right)),
            (self.pe.at[0], self.dg.at[3], (up, left)),
            (self.pe.at[0], self.dg.at[2], (up, right)),
            (self.pe.at[1], self.dg.at[1], (down, left)),
            (self.pe.at[1], self.dg.at[0], (down, right)),
        )
        self.copies = [
            pltpu.make_async_remote_copy(
                src_ref=src,
                dst_ref=dst,
                send_sem=self.ss.at[n],
                recv_sem=self.rs.at[n],
                device_id=device,
                device_id_type=MESH,
            )
            for n, (src, dst, device) in enumerate(plan)
        ]
        for copy in self.copies[0:2]:
            copy.start()
        packed = levels() if callable(levels) else levels
        self.pe[0] = packed[0:8]
        self.pe[1] = packed[rows - 8 : rows]
        for copy in self.copies[4:8]:
            copy.start()
        tall = packed
        if rows < LANES:
            tall = jnp.concatenate([packed, jnp.zeros((LANES - rows, LANES), F32)], axis=0)
        turned = tall.T
        cs = self.ptl.shape[0]
        self.ptl[...] = turned[0:cs]
        self.ptr[...] = turned[64 : 64 + cs]
        self.pk[...] = packed
        for copy in self.copies[2:4]:
            copy.start()

    def arrive(self):
        for copy in self.copies:
            copy.wait_recv()
        rows = self.rows
        lane = iota((1, LANES), 1)
        low = lane < 64
        self.has_top, self.has_bot = self.gx > 0, self.gx < self.ngx - 1
        edge = jnp.where(low, jnp.where(self.gy > 0, 1, 0), jnp.where(self.gy < self.ngy - 1, 1, 0)) > 0
        cs = self.cl.shape[0]
        fill = jnp.zeros((64 - cs, LANES), F32)
        turned = jnp.concatenate([self.cl[...], fill, self.cr[...], fill], axis=0)
        sides = turned.T[0:rows]
        above = jnp.where(low, pltpu.roll(self.dg[0], 64, 1), pltpu.roll(self.dg[1], 64, 1))
        below = jnp.where(low, pltpu.roll(self.dg[2], 64, 1), pltpu.roll(self.dg[3], 64, 1))
        above = jnp.where(self.has_top, above, 0.0)
        below = jnp.where(self.has_bot, below, 0.0)
        rim = jnp.where(edge, jnp.concatenate([above, sides, below], axis=0), 0.0)
        total = rows + 16
        up = pltpu.roll(rim, 1, 0)[8 : rows + 8]
        down = pltpu.roll(rim, total - 1, 0)[8 : rows + 8]
        near = sides + self.pk[...]
        beside = jnp.where(low, pltpu.roll(near, 1, 1), pltpu.roll(near, LANES - 1, 1))
        mid = sides + RATE * (up + down + beside - 4.0 * sides)
        self.rim, self.mid = rim, jnp.where(edge, mid, 0.0)

    def two_steps(self, n, field, rim_ref, mid_ref):
        rows = self.rows
        total = rows + 16
        rim, rim_mid = rim_ref[...], mid_ref[...]
        top = jnp.where(self.has_top, self.top[n], 0.0)
        bot = jnp.where(self.has_bot, self.bot[n], 0.0)
        whole = jnp.concatenate([top, field, bot], axis=0)
        lane, row = iota((total, LANES), 1), iota((total, LANES), 0)
        to_first, to_last = LANES - 1 - 2 * n, 63 - 2 * n
        beside = (
            jnp.where(lane == 0, pltpu.roll(rim, to_first, 1), pltpu.roll(whole, 1, 1))
            + jnp.where(lane == LANES - 1, pltpu.roll(rim, to_last, 1), pltpu.roll(whole, LANES - 1, 1))
            + pltpu.roll(whole, 1, 0)
            + pltpu.roll(whole, total - 1, 0)
        )
        mid = whole + RATE * (beside - 4.0 * whole)
        first_row, last_row = jnp.where(self.has_top, 0, 8), jnp.where(self.has_bot, total, rows + 8)
        mid = jnp.where((row >= first_row) & (row < last_row), mid, 0.0)
        own = mid[8 : rows + 8]
        lane = iota((rows, LANES), 1)
        beside = (
            jnp.where(lane == 0, pltpu.roll(rim_mid, to_first, 1), pltpu.roll(own, 1, 1))
            + jnp.where(lane == LANES - 1, pltpu.roll(rim_mid, to_last, 1), pltpu.roll(own, LANES - 1, 1))
            + pltpu.roll(mid, 1, 0)[8 : rows + 8]
            + pltpu.roll(mid, total - 1, 0)[8 : rows + 8]
        )
        return own + RATE * (beside - 4.0 * own)

    def wait_sent(self):
        for copy in self.copies:
            copy.wait_send()


def kernel(
    sizes,
    atm_hbm,
    ocean_hbm,
    coef_hbm,
    mix_hbm,
    share_hbm,
    src_hbm,
    dest_hbm,
    owner_hbm,
    final_hbm,
    aerial_ref,
    atm_ref,
    coef_ref,
    mix_ref,
    src_ref,
    dest_ref,
    owner_ref,
    share,
    ocean,
    final,
    surf,
    mixed,
    lists,
    table,
    table_s,
    id_send,
    id_recv,
    f_send,
    f_recv,
    hits,
    spread,
    pick,
    s_send,
    s_recv,
    home_lines,
    rims,
    mids,
    in_sems,
    table_sem,
    final_sem,
    id_ss,
    id_rs,
    f_ss,
    f_rs,
    s_ss,
    s_rs,
    *halo_refs,
):
    ngx, nx, nz = sizes
    ngy = nx * nz
    slots = ngy * CAP
    chunks = ngy // CHUNK
    la, ra = atm_ref.shape[0], atm_ref.shape[1]
    lo, ro = ocean.shape[0], ocean.shape[1]
    nb = src_ref.shape[1]
    fluxes = coef_ref.shape[1]
    gx, gy = lax.axis_index("gx"), lax.axis_index("gy")
    my_x, my_z = lax.div(gy, nz), lax.rem(gy, nz)
    place = (gx, gy, ngx, ngy)

    loads = [
        pltpu.make_async_copy(far, near, in_sems.at[n])
        for n, (far, near) in enumerate(
            (
                (owner_hbm, owner_ref),
                (dest_hbm, dest_ref),
                (atm_hbm, atm_ref),
                (coef_hbm, coef_ref),
                (mix_hbm, mix_ref),
                (src_hbm, src_ref),
                (share_hbm.at[0], share),
                (ocean_hbm, ocean),
            )
        )
    ]
    for load in loads:
        load.start()

    def shift(i):
        k = lax.div(i, nx)
        dx = lax.rem(i, nx)
        dz = lax.div(k + 1, 2) * (2 * lax.rem(k, 2) - 1)
        return dx, dz

    def ahead(i):
        dx, dz = shift(i)
        return lax.rem(my_x + dx, nx) * nz + lax.rem(my_z + dz + nz, nz)

    def behind(i):
        dx, dz = shift(i)
        return lax.rem(my_x - dx + nx, nx) * nz + lax.rem(my_z - dz + nz, nz)

    def to_all(act):
        def burst(t, carry):
            for u in range(BURST):
                act(ngy - 1 - BURST * t - u)
            return carry

        lax.fori_loop(0, ngy // BURST - 1, burst, 0)
        for i in reversed(range(1, BURST)):
            act(i)

    barrier = pltpu.get_barrier_semaphore()
    up, down = lax.rem(gx + ngx - 1, ngx), lax.rem(gx + 1, ngx)
    left, right = lax.rem(gy + ngy - 1, ngy), lax.rem(gy + 1, ngy)
    for device in ((up, gy), (down, gy), (up, left), (up, right), (down, left), (down, right)):
        pl.semaphore_signal(barrier, inc=1, device_id=device, device_id_type=MESH)

    to_all(lambda i: pl.semaphore_signal(barrier, inc=1, device_id=(gx, ahead(i)), device_id_type=MESH))

    atm_halo = Halo(place, halo_refs[0:11], ra, la)
    top_halo = Halo(place, halo_refs[11:22], ro, 1)
    low_halo = Halo(place, halo_refs[22:33], ro, lo - 1)

    for load in loads[0:3]:
        load.wait()
    lists[...] = jnp.full((8, LANES), -1, I32)
    lists[0:1, 0:nb] = owner_ref[...]
    lists[1:2, 0:nb] = dest_ref[...]
    own_row, dest_row = lists[0:1, :], lists[1:2, :]
    lane = iota((1, LANES), 1)
    own_x = jnp.zeros((1, LANES), I32)
    for t in range(1, nx):
        own_x = own_x + jnp.where(own_row >= t * nz, 1, 0)
    own_z = own_row - own_x * nz
    dx = own_x - my_x
    dx = jnp.where(dx < 0, dx + nx, dx)
    dz = own_z - my_z
    dz = jnp.where(dz < 0, dz + nz, dz)
    k = jnp.where(dz == 0, 0, jnp.where(dz <= nz // 2, 2 * dz - 1, 2 * (nz - dz)))
    step_row = k * nx + dx
    sq = (LANES, LANES)
    sub_q, lane_q = iota(sq, 0), iota(sq, 1)
    own_sq = jnp.broadcast_to(own_row, sq)
    same = (own_sq == own_sq.T) & (sub_q < lane_q)
    rank = jnp.sum(jnp.where(same, 1, 0), axis=0, keepdims=True)
    slot_row = jnp.where(lane < nb, step_row * CAP + rank, -1)
    slot_col = jnp.broadcast_to(slot_row, sq).T
    table[...] = jnp.zeros((8, LANES), I32)
    table[0:1, :] = jnp.clip(slot_row, 0, slots - 1)
    for b in range(-(-slots // LANES)):
        hit = slot_col == lane_q + b * LANES
        block = jnp.sum(jnp.where(hit, sub_q, 0), axis=0, keepdims=True)
        table[1 + b : 2 + b, :] = jnp.clip(block, 0, nb - 1)
    table_copy = pltpu.make_async_copy(table, table_s, table_sem)
    table_copy.start()
    wide = (ngy, LANES)
    step_i, lane_i = iota(wide, 0), iota(wide, 1)
    slot_w = jnp.broadcast_to(slot_row, wide)
    line_w = jnp.broadcast_to((dest_row + 1).astype(F32), wide)
    ids = jnp.zeros(wide, F32)
    for j in range(CAP):
        line = jnp.sum(jnp.where(slot_w == step_i * CAP + j, line_w, 0.0), axis=1, keepdims=True)
        ids = jnp.where(lax.rem(lane_i, CAP) == j, jnp.broadcast_to(line, wide), ids)
    ids = jnp.where(lax.div(lane_i, SPAN) == lax.rem(step_i, CHUNK), ids, 0.0)
    id_send[...] = ids.reshape(ngy, 1, LANES)
    id_recv[0] = id_send[0]

    atm_packed = pack_sides([atm_ref[l] for l in range(la)], ra)

    pl.semaphore_wait(barrier, ngy - 1 + 6)

    atm_halo.start(atm_ref, atm_packed)

    def id_copy(i):
        return pltpu.make_async_remote_copy(
            src_ref=id_send.at[i],
            dst_ref=id_recv.at[i],
            send_sem=id_ss,
            recv_sem=id_rs,
            device_id=(gx, ahead(i)),
            device_id_type=MESH,
        )

    to_all(lambda i: id_copy(i).start())

    atm_halo.arrive()
    rims[0, 0 : ra + 16] = atm_halo.rim
    mids[0, 0:ra] = atm_halo.mid

    for l in range(la):
        surf[l] = atm_halo.two_steps(l, atm_ref[l], rims.at[0, 0 : ra + 16], mids.at[0, 0:ra])

    for load in loads[3:5]:
        load.wait()

    band = 16

    def flux_band(c, carry):
        r0 = pl.multiple_of(c * band, band)
        fields = [surf[l, pl.ds(r0, band)] for l in range(la)]
        flux = []
        for kk in range(fluxes):
            total = coef_ref[0, kk] * fields[0]
            for l in range(1, la):
                total = total + coef_ref[l, kk] * fields[l]
            flux.append(jnp.tanh(total).astype(BF16).astype(F32))
        for l in range(lo):
            total = mix_ref[l, 0] * flux[0]
            for kk in range(1, fluxes):
                total = total + mix_ref[l, kk] * flux[kk]
            total = 0.5 * total
            for j in range(CAP):
                mixed[pl.ds(pl.multiple_of((l * CAP + j) * ra + r0, band), band)] = total
        return carry

    lax.fori_loop(0, ra // band, flux_band, 0)

    table_copy.wait()
    for load in loads[5:7]:
        load.wait()

    used = lo * CAP
    slot_of_row = lax.rem(iota((used, LANES), 0), CAP)

    def f_copy(i):
        return pltpu.make_async_remote_copy(
            src_ref=f_send.at[i],
            dst_ref=f_recv.at[i],
            send_sem=f_ss,
            recv_sem=f_rs.at[lax.div(i, CHUNK)],
            device_id=(gx, ahead(i)),
            device_id_type=MESH,
        )

    def contribution(i):
        left_parts, right_parts = [], []
        for j in range(CAP):
            s = i * CAP + j
            q = jnp.clip(table_s[1 + lax.div(s, LANES), lax.rem(s, LANES)], 0, nb - 1)
            rows = mixed[pl.ds(src_ref[0, q], used, stride=ra), :]
            rows = jnp.where(slot_of_row == j, rows, 0.0)
            left_parts.append(rows.astype(BF16))
            right_parts.append(share[q])
        return jnp.dot(
            jnp.concatenate(left_parts, axis=1),
            jnp.concatenate(right_parts, axis=0),
            preferred_element_type=F32,
        ).astype(BF16)

    def send_blocks(t, carry):
        last = ngy - 1 - UNROLL * t
        steps = [last - u for u in range(UNROLL)]
        for i, blocks in zip(steps, [contribution(i) for i in steps]):
            f_send[i] = blocks
            f_copy(i).start()
        return carry

    lax.fori_loop(0, ngy // UNROLL - 1, send_blocks, 0)
    nearest = [contribution(i) for i in range(UNROLL)]
    for i in reversed(range(1, UNROLL)):
        f_send[i] = nearest[i]
        f_copy(i).start()
    f_recv[0] = nearest[0]

    pltpu.make_async_remote_copy(
        src_ref=id_send.at[1:ngy],
        dst_ref=id_recv.at[1:ngy],
        send_sem=id_ss,
        recv_sem=id_rs,
        device_id=(gx, gy),
        device_id_type=MESH,
    ).wait_recv()
    line_of_row = iota((ro, LANES), 0) + 1
    level_of_lane = lax.rem(lax.div(iota((ro, LANES), 1), CAP), GROUP)
    for c in range(chunks):
        ids_row = id_recv[c * CHUNK]
        for t in range(1, CHUNK):
            ids_row = ids_row + id_recv[c * CHUNK + t]
        hit = jnp.where(jnp.broadcast_to(ids_row.astype(I32), (ro, LANES)) == line_of_row, 1.0, 0.0)
        hits[:, c * LANES : (c + 1) * LANES] = hit.astype(BF16)
        for l in range(GROUP):
            spread[c, l * ro : (l + 1) * ro, :] = jnp.where(level_of_lane == l, hit, 0.0).astype(BF16)
    chosen = iota((slots, ngy * SPAN), 0)
    chosen = jnp.where(
        iota((slots, ngy * SPAN), 1) == lax.div(chosen, CAP) * SPAN + lax.rem(chosen, CAP), 1.0, 0.0
    ).astype(BF16)
    pick[...] = lax.dot_general(chosen, hits[...], NT, preferred_element_type=F32).astype(BF16)

    loads[7].wait()

    def land(c, l0, l1):
        base = GROUP * (l0 // GROUP)
        rows = f_recv[c * CHUNK : (c + 1) * CHUNK, base * CAP : base * CAP + SPAN, :]
        landed = jnp.dot(
            spread[c, (l0 - base) * ro : (l1 - base) * ro, :],
            rows.reshape(LANES, LANES),
            preferred_element_type=F32,
        )
        for l in range(l0, l1):
            ocean[l] = ocean[l] + landed[(l - l0) * ro : (l - l0 + 1) * ro]

    for c in reversed(range(chunks)):
        first = 1 if c == 0 else c * CHUNK
        here = pl.ds(first, (c + 1) * CHUNK - first)
        pltpu.make_async_remote_copy(
            src_ref=f_send.at[here],
            dst_ref=f_recv.at[here],
            send_sem=f_ss,
            recv_sem=f_rs.at[c],
            device_id=(gx, gy),
            device_id_type=MESH,
        ).wait_recv()
        if c:
            for l0 in range(0, lo, GROUP):
                land(c, l0, l0 + GROUP)
    land(0, 0, 1)
    top_halo.start(ocean.at[0:1], lambda: pack_sides([ocean[0]], ro))
    land(0, 1, GROUP)
    for l0 in range(GROUP, lo, GROUP):
        land(0, l0, l0 + GROUP)
    low_halo.start(ocean.at[1:lo], lambda: pack_sides([ocean[l] for l in range(1, lo)], ro))

    top_halo.arrive()
    rims[1] = top_halo.rim
    mids[1] = top_halo.mid
    skin = top_halo.two_steps(0, ocean[0], rims.at[1], mids.at[1])
    final[0] = skin
    lines = jnp.dot(pick[...], skin.astype(BF16), preferred_element_type=F32)
    s_send[...] = lines.reshape(ngy, CAP, LANES)
    s_recv[0] = s_send[0]

    def s_copy(i):
        return pltpu.make_async_remote_copy(
            src_ref=s_send.at[i],
            dst_ref=s_recv.at[i],
            send_sem=s_ss,
            recv_sem=s_rs,
            device_id=(gx, behind(i)),
            device_id_type=MESH,
        )

    to_all(lambda i: s_copy(i).start())

    low_halo.arrive()
    rims[2] = low_halo.rim
    mids[2] = low_halo.mid

    def low_level(n, carry):
        final[n + 1] = low_halo.two_steps(n, ocean[n + 1], rims.at[2], mids.at[2])
        return carry

    lax.fori_loop(0, lo - 1, low_level, 0)
    final_copy = pltpu.make_async_copy(final, final_hbm, final_sem)
    final_copy.start()

    rest = pl.ds(1, ngy - 1)
    pltpu.make_async_remote_copy(
        src_ref=s_send.at[rest],
        dst_ref=s_recv.at[rest],
        send_sem=s_ss,
        recv_sem=s_rs,
        device_id=(gx, gy),
        device_id_type=MESH,
    ).wait_recv()
    home_lines[...] = s_recv[...].reshape(slots, 1, LANES)
    row_a = iota((ra, LANES), 0)

    def home(b, total):
        return sum([part(b * UNROLL + u) for u in range(UNROLL)], total)

    def part(b):
        left_parts, right_parts = [], []
        for j in range(4):
            q = b * 4 + j
            line = jnp.broadcast_to(home_lines[jnp.clip(table_s[0, q], 0, slots - 1)], (ra, LANES))
            left_parts.append(jnp.where(row_a == src_ref[0, q], line, 0.0).astype(BF16))
            right_parts.append(share[q])
        return lax.dot_general(
            jnp.concatenate(left_parts, axis=1),
            jnp.concatenate(right_parts, axis=1),
            NT,
            preferred_element_type=F32,
        )

    aerial_ref[...] = lax.fori_loop(0, nb // (4 * UNROLL), home, jnp.zeros((ra, LANES), F32))

    for halo in (atm_halo, top_halo, low_halo):
        halo.wait_sent()
    for buffer, sem, first in ((id_send, id_ss, 1), (f_send, f_ss, 1), (s_send, s_ss, 1)):
        here = pl.ds(first, buffer.shape[0] - first)
        pltpu.make_async_remote_copy(
            src_ref=buffer.at[here],
            dst_ref=buffer.at[here],
            send_sem=sem,
            recv_sem=s_rs,
            device_id=(gx, gy),
            device_id_type=MESH,
        ).wait_send()
    final_copy.wait()


def halo_scratch(rows, count):
    cs = -(-2 * count // 8) * 8
    return [
        pltpu.VMEM((count, 8, LANES), F32),
        pltpu.VMEM((count, 8, LANES), F32),
        pltpu.VMEM((cs, LANES), F32),
        pltpu.VMEM((cs, LANES), F32),
        pltpu.VMEM((4, 8, LANES), F32),
        pltpu.VMEM((cs, LANES), F32),
        pltpu.VMEM((cs, LANES), F32),
        pltpu.VMEM((2, 8, LANES), F32),
        pltpu.VMEM((rows, LANES), F32),
        pltpu.SemaphoreType.DMA((8,)),
        pltpu.SemaphoreType.DMA((8,)),
    ]


def body(sizes, atm_state, ocean_temp, flux_coef, flux_mix, share, src, dest, owner):
    ngx, nx, nz = sizes
    ngy = nx * nz
    slots = ngy * CAP
    la, ra, _ = atm_state.shape
    lo, ro, _ = ocean_temp.shape
    nb = src.shape[1]
    vmem = pl.BlockSpec(memory_space=pltpu.VMEM)
    far = pl.BlockSpec(memory_space=pltpu.HBM)
    dma = pltpu.SemaphoreType.DMA
    return pl.pallas_call(
        functools.partial(kernel, sizes),
        out_shape=(
            jax.ShapeDtypeStruct(ocean_temp.shape, F32),
            jax.ShapeDtypeStruct((ra, LANES), F32),
        ),
        in_specs=[far] * 8,
        out_specs=(far, vmem),
        scratch_shapes=[
            pltpu.VMEM(atm_state.shape, F32),
            pltpu.SMEM(flux_coef.shape[::-1], F32),
            pltpu.SMEM(flux_mix.shape, F32),
            pltpu.SMEM((1, nb), I32),
            pltpu.VMEM((1, nb), I32),
            pltpu.VMEM((1, nb), I32),
            pltpu.VMEM((nb, LANES, LANES), BF16),
            pltpu.VMEM((lo, ro, LANES), F32),
            pltpu.VMEM((lo, ro, LANES), F32),
            pltpu.VMEM((la, ra, LANES), F32),
            pltpu.VMEM((lo * CAP * ra, LANES), F32),
            pltpu.VMEM((8, LANES), I32),
            pltpu.VMEM((8, LANES), I32),
            pltpu.SMEM((8, LANES), I32),
            pltpu.VMEM((ngy, 1, LANES), F32),
            pltpu.VMEM((ngy, 1, LANES), F32),
            pltpu.VMEM((ngy, lo * CAP, LANES), BF16),
            pltpu.VMEM((ngy, lo * CAP, LANES), BF16),
            pltpu.VMEM((ro, ngy * SPAN), BF16),
            pltpu.VMEM((ngy // CHUNK, GROUP * ro, LANES), BF16),
            pltpu.VMEM((slots, ro), BF16),
            pltpu.VMEM((ngy, CAP, LANES), F32),
            pltpu.VMEM((ngy, CAP, LANES), F32),
            pltpu.VMEM((slots, 1, LANES), F32),
            pltpu.VMEM((3, ro + 16, LANES), F32),
            pltpu.VMEM((3, ro, LANES), F32),
            dma((8,)),
            dma,
            dma,
            dma,
            dma,
            dma,
            dma((ngy // CHUNK,)),
            dma,
            dma,
            *halo_scratch(ra, la),
            *halo_scratch(ro, 1),
            *halo_scratch(ro, lo - 1),
        ],
        compiler_params=pltpu.CompilerParams(
            collective_id=0, has_side_effects=True, vmem_limit_bytes=60 * 1024 * 1024
        ),
        cost_estimate=pl.CostEstimate(flops=200_000_000, bytes_accessed=5_000_000, transcendentals=100_000),
    )(atm_state, ocean_temp, flux_coef.T, flux_mix, share, src, dest, owner.reshape(1, nb))


def solution(mesh):
    ngy = mesh.shape["gy"]
    nx = 4
    return jax.shard_map(
        functools.partial(body, (mesh.shape["gx"], nx, ngy // nx)),
        mesh=mesh,
        in_specs=(
            P(None, "gx", "gy"),
            P(None, "gx", "gy"),
            P(),
            P(),
            P("gx", "gy", None, None),
            P("gx", "gy"),
            P("gx", "gy"),
            P("gx", "gy", None),
        ),
        out_specs=(P(None, "gx", "gy"), P("gx", "gy")),
        check_vma=False,
    )
```

```python
import functools

import jax
import jax.numpy as jnp
from jax import lax
from jax.experimental import pallas as pl
from jax.experimental.pallas import tpu as pltpu
from jax.sharding import PartitionSpec as P

MESH = pl.DeviceIdType.MESH
RATE = 0.2
CAP = 4
F32, BF16, I32 = jnp.float32, jnp.bfloat16, jnp.int32
LANES = 128
NT = (((1,), (1,)), ((), ()))
GROUP = 2
SPAN = GROUP * CAP
CHUNK = LANES // SPAN
UNROLL = 4
BURST = 8


def iota(shape, dim):
    return lax.broadcasted_iota(I32, shape, dim)


def pack_sides(levels, rows):
    pair = lax.shift_right_logical(iota((rows, LANES), 1), 1)
    packed = jnp.zeros((rows, LANES), F32)
    for n, field in enumerate(levels):
        packed = jnp.where(pair == n, pltpu.roll(field, 2 * n, 1) if n else field, packed)
        packed = jnp.where(pair == 32 + n, pltpu.roll(field, 66 + 2 * n, 1), packed)
    return packed


class Halo:
    def __init__(self, place, refs, rows, count):
        self.gx, self.gy, self.ngx, self.ngy = place
        (self.top, self.bot, self.cl, self.cr, self.dg, self.ptl, self.ptr, self.pe, self.pk, self.ss, self.rs) = refs
        self.rows, self.count = rows, count

    def start(self, field, levels):
        rows = self.rows
        up, down = lax.rem(self.gx + self.ngx - 1, self.ngx), lax.rem(self.gx + 1, self.ngx)
        left, right = lax.rem(self.gy + self.ngy - 1, self.ngy), lax.rem(self.gy + 1, self.ngy)
        plan = (
            (field.at[:, 0:8], self.bot, (up, self.gy)),
            (field.at[:, rows - 8 : rows], self.top, (down, self.gy)),
            (self.ptl, self.cr, (self.gx, left)),
            (self.ptr, self.cl, (self.gx, right)),
            (self.pe.at[0], self.dg.at[3], (up, left)),
            (self.pe.at[0], self.dg.at[2], (up, right)),
            (self.pe.at[1], self.dg.at[1], (down, left)),
            (self.pe.at[1], self.dg.at[0], (down, right)),
        )
        self.copies = [
            pltpu.make_async_remote_copy(
                src_ref=src,
                dst_ref=dst,
                send_sem=self.ss.at[n],
                recv_sem=self.rs.at[n],
                device_id=device,
                device_id_type=MESH,
            )
            for n, (src, dst, device) in enumerate(plan)
        ]
        for copy in self.copies[0:2]:
            copy.start()
        packed = levels() if callable(levels) else levels
        self.pe[0] = packed[0:8]
        self.pe[1] = packed[rows - 8 : rows]
        for copy in self.copies[4:8]:
            copy.start()
        tall = packed
        if rows < LANES:
            tall = jnp.concatenate([packed, jnp.zeros((LANES - rows, LANES), F32)], axis=0)
        turned = tall.T
        cs = self.ptl.shape[0]
        self.ptl[...] = turned[0:cs]
        self.ptr[...] = turned[64 : 64 + cs]
        self.pk[...] = packed
        for copy in self.copies[2:4]:
            copy.start()

    def arrive(self):
        for copy in self.copies:
            copy.wait_recv()
        rows = self.rows
        lane = iota((1, LANES), 1)
        low = lane < 64
        self.has_top, self.has_bot = self.gx > 0, self.gx < self.ngx - 1
        edge = jnp.where(low, jnp.where(self.gy > 0, 1, 0), jnp.where(self.gy < self.ngy - 1, 1, 0)) > 0
        cs = self.cl.shape[0]
        fill = jnp.zeros((64 - cs, LANES), F32)
        turned = jnp.concatenate([self.cl[...], fill, self.cr[...], fill], axis=0)
        sides = turned.T[0:rows]
        above = jnp.where(low, pltpu.roll(self.dg[0], 64, 1), pltpu.roll(self.dg[1], 64, 1))
        below = jnp.where(low, pltpu.roll(self.dg[2], 64, 1), pltpu.roll(self.dg[3], 64, 1))
        above = jnp.where(self.has_top, above, 0.0)
        below = jnp.where(self.has_bot, below, 0.0)
        rim = jnp.where(edge, jnp.concatenate([above, sides, below], axis=0), 0.0)
        total = rows + 16
        up = pltpu.roll(rim, 1, 0)[8 : rows + 8]
        down = pltpu.roll(rim, total - 1, 0)[8 : rows + 8]
        near = sides + self.pk[...]
        beside = jnp.where(low, pltpu.roll(near, 1, 1), pltpu.roll(near, LANES - 1, 1))
        mid = sides + RATE * (up + down + beside - 4.0 * sides)
        mid = jnp.where(edge, mid, 0.0)
        odd = lax.rem(lane, 2) == 1
        self.rim = jnp.where(odd, rim, pltpu.roll(rim, 64, 1))
        self.mid = jnp.where(odd, mid, pltpu.roll(mid, 64, 1))

    def two_steps(self, n, field, rim_ref, mid_ref):
        rows = self.rows
        total = rows + 16
        rim, rim_mid = rim_ref[...], mid_ref[...]
        top = jnp.where(self.has_top, self.top[n], 0.0)
        bot = jnp.where(self.has_bot, self.bot[n], 0.0)
        whole = jnp.concatenate([top, field, bot], axis=0)
        lane, row = iota((total, LANES), 1), iota((total, LANES), 0)
        to_ends = LANES - 1 - 2 * n
        side = pltpu.roll(rim, to_ends, 1)
        beside = (
            jnp.where(lane == 0, side, pltpu.roll(whole, 1, 1))
            + jnp.where(lane == LANES - 1, side, pltpu.roll(whole, LANES - 1, 1))
            + pltpu.roll(whole, 1, 0)
            + pltpu.roll(whole, total - 1, 0)
        )
        mid = whole + RATE * (beside - 4.0 * whole)
        first_row, last_row = jnp.where(self.has_top, 0, 8), jnp.where(self.has_bot, total, rows + 8)
        mid = jnp.where((row >= first_row) & (row < last_row), mid, 0.0)
        own = mid[8 : rows + 8]
        lane = iota((rows, LANES), 1)
        side = pltpu.roll(rim_mid, to_ends, 1)
        beside = (
            jnp.where(lane == 0, side, pltpu.roll(own, 1, 1))
            + jnp.where(lane == LANES - 1, side, pltpu.roll(own, LANES - 1, 1))
            + pltpu.roll(mid, 1, 0)[8 : rows + 8]
            + pltpu.roll(mid, total - 1, 0)[8 : rows + 8]
        )
        return own + RATE * (beside - 4.0 * own)

    def wait_sent(self):
        for copy in self.copies:
            copy.wait_send()


def kernel(
    sizes,
    atm_hbm,
    ocean_hbm,
    coef_hbm,
    mix_hbm,
    share_hbm,
    src_hbm,
    dest_hbm,
    owner_hbm,
    final_hbm,
    aerial_ref,
    atm_ref,
    coef_ref,
    mix_ref,
    src_ref,
    dest_ref,
    owner_ref,
    share,
    ocean,
    final,
    surf,
    mixed,
    lists,
    table,
    table_s,
    id_send,
    id_recv,
    f_send,
    f_recv,
    hits,
    spread,
    pick,
    s_send,
    s_recv,
    home_lines,
    rims,
    mids,
    in_sems,
    table_sem,
    final_sem,
    id_ss,
    id_rs,
    f_ss,
    f_rs,
    s_ss,
    s_rs,
    *halo_refs,
):
    ngx, nx, nz = sizes
    ngy = nx * nz
    slots = ngy * CAP
    chunks = ngy // CHUNK
    la, ra = atm_ref.shape[0], atm_ref.shape[1]
    lo, ro = ocean.shape[0], ocean.shape[1]
    nb = src_ref.shape[1]
    fluxes = coef_ref.shape[1]
    gx, gy = lax.axis_index("gx"), lax.axis_index("gy")
    my_x, my_z = lax.div(gy, nz), lax.rem(gy, nz)
    place = (gx, gy, ngx, ngy)

    loads = [
        pltpu.make_async_copy(far, near, in_sems.at[n])
        for n, (far, near) in enumerate(
            (
                (owner_hbm, owner_ref),
                (dest_hbm, dest_ref),
                (atm_hbm, atm_ref),
                (coef_hbm, coef_ref),
                (mix_hbm, mix_ref),
                (src_hbm, src_ref),
                (share_hbm.at[0], share),
                (ocean_hbm, ocean),
            )
        )
    ]
    for load in loads:
        load.start()

    def shift(i):
        k = lax.div(i, nx)
        dx = lax.rem(i, nx)
        dz = lax.div(k + 1, 2) * (2 * lax.rem(k, 2) - 1)
        return dx, dz

    def ahead(i):
        dx, dz = shift(i)
        return lax.rem(my_x + dx, nx) * nz + lax.rem(my_z + dz + nz, nz)

    def behind(i):
        dx, dz = shift(i)
        return lax.rem(my_x - dx + nx, nx) * nz + lax.rem(my_z - dz + nz, nz)

    def to_all(act):
        def burst(t, carry):
            for u in range(BURST):
                act(ngy - 1 - BURST * t - u)
            return carry

        lax.fori_loop(0, ngy // BURST - 1, burst, 0)
        for i in reversed(range(1, BURST)):
            act(i)

    barrier = pltpu.get_barrier_semaphore()
    up, down = lax.rem(gx + ngx - 1, ngx), lax.rem(gx + 1, ngx)
    left, right = lax.rem(gy + ngy - 1, ngy), lax.rem(gy + 1, ngy)
    for device in ((up, gy), (down, gy), (up, left), (up, right), (down, left), (down, right)):
        pl.semaphore_signal(barrier, inc=1, device_id=device, device_id_type=MESH)

    to_all(lambda i: pl.semaphore_signal(barrier, inc=1, device_id=(gx, ahead(i)), device_id_type=MESH))

    atm_halo = Halo(place, halo_refs[0:11], ra, la)
    top_halo = Halo(place, halo_refs[11:22], ro, 1)
    low_halo = Halo(place, halo_refs[22:33], ro, lo - 1)

    for load in loads[0:3]:
        load.wait()
    lists[...] = jnp.full((8, LANES), -1, I32)
    lists[0:1, 0:nb] = owner_ref[...]
    lists[1:2, 0:nb] = dest_ref[...]
    own_row, dest_row = lists[0:1, :], lists[1:2, :]
    lane = iota((1, LANES), 1)
    own_x = jnp.zeros((1, LANES), I32)
    for t in range(1, nx):
        own_x = own_x + jnp.where(own_row >= t * nz, 1, 0)
    own_z = own_row - own_x * nz
    dx = own_x - my_x
    dx = jnp.where(dx < 0, dx + nx, dx)
    dz = own_z - my_z
    dz = jnp.where(dz < 0, dz + nz, dz)
    k = jnp.where(dz == 0, 0, jnp.where(dz <= nz // 2, 2 * dz - 1, 2 * (nz - dz)))
    step_row = k * nx + dx
    sq = (LANES, LANES)
    sub_q, lane_q = iota(sq, 0), iota(sq, 1)
    own_sq = jnp.broadcast_to(own_row, sq)
    same = (own_sq == own_sq.T) & (sub_q < lane_q)
    rank = jnp.sum(jnp.where(same, 1, 0), axis=0, keepdims=True)
    slot_row = jnp.where(lane < nb, step_row * CAP + rank, -1)
    slot_col = jnp.broadcast_to(slot_row, sq).T
    table[...] = jnp.zeros((8, LANES), I32)
    table[0:1, :] = jnp.clip(slot_row, 0, slots - 1)
    for b in range(-(-slots // LANES)):
        hit = slot_col == lane_q + b * LANES
        block = jnp.sum(jnp.where(hit, sub_q, 0), axis=0, keepdims=True)
        table[1 + b : 2 + b, :] = jnp.clip(block, 0, nb - 1)
    table_copy = pltpu.make_async_copy(table, table_s, table_sem)
    table_copy.start()
    wide = (ngy, LANES)
    step_i, lane_i = iota(wide, 0), iota(wide, 1)
    slot_w = jnp.broadcast_to(slot_row, wide)
    line_w = jnp.broadcast_to((dest_row + 1).astype(F32), wide)
    ids = jnp.zeros(wide, F32)
    for j in range(CAP):
        line = jnp.sum(jnp.where(slot_w == step_i * CAP + j, line_w, 0.0), axis=1, keepdims=True)
        ids = jnp.where(lax.rem(lane_i, CAP) == j, jnp.broadcast_to(line, wide), ids)
    ids = jnp.where(lax.div(lane_i, SPAN) == lax.rem(step_i, CHUNK), ids, 0.0)
    id_send[...] = ids.reshape(ngy, 1, LANES)
    id_recv[0] = id_send[0]

    atm_packed = pack_sides([atm_ref[l] for l in range(la)], ra)

    pl.semaphore_wait(barrier, ngy - 1 + 6)

    atm_halo.start(atm_ref, atm_packed)

    def id_copy(i):
        return pltpu.make_async_remote_copy(
            src_ref=id_send.at[i],
            dst_ref=id_recv.at[i],
            send_sem=id_ss,
            recv_sem=id_rs,
            device_id=(gx, ahead(i)),
            device_id_type=MESH,
        )

    to_all(lambda i: id_copy(i).start())

    atm_halo.arrive()
    rims[0, 0 : ra + 16] = atm_halo.rim
    mids[0, 0:ra] = atm_halo.mid

    for l in range(la):
        surf[l] = atm_halo.two_steps(l, atm_ref[l], rims.at[0, 0 : ra + 16], mids.at[0, 0:ra])

    for load in loads[3:5]:
        load.wait()

    band = 16

    def flux_band(c, carry):
        r0 = pl.multiple_of(c * band, band)
        fields = [surf[l, pl.ds(r0, band)] for l in range(la)]
        flux = []
        for kk in range(fluxes):
            total = coef_ref[0, kk] * fields[0]
            for l in range(1, la):
                total = total + coef_ref[l, kk] * fields[l]
            flux.append(jnp.tanh(total).astype(BF16).astype(F32))
        for l in range(lo):
            total = mix_ref[l, 0] * flux[0]
            for kk in range(1, fluxes):
                total = total + mix_ref[l, kk] * flux[kk]
            total = 0.5 * total
            for j in range(CAP):
                mixed[pl.ds(pl.multiple_of((l * CAP + j) * ra + r0, band), band)] = total
        return carry

    lax.fori_loop(0, ra // band, flux_band, 0)

    table_copy.wait()
    for load in loads[5:7]:
        load.wait()

    used = lo * CAP
    slot_of_row = lax.rem(iota((used, LANES), 0), CAP)

    def f_copy(i):
        return pltpu.make_async_remote_copy(
            src_ref=f_send.at[i],
            dst_ref=f_recv.at[i],
            send_sem=f_ss,
            recv_sem=f_rs.at[lax.div(i, CHUNK)],
            device_id=(gx, ahead(i)),
            device_id_type=MESH,
        )

    def contribution(i):
        left_parts, right_parts = [], []
        for j in range(CAP):
            s = i * CAP + j
            q = jnp.clip(table_s[1 + lax.div(s, LANES), lax.rem(s, LANES)], 0, nb - 1)
            rows = mixed[pl.ds(src_ref[0, q], used, stride=ra), :]
            rows = jnp.where(slot_of_row == j, rows, 0.0)
            left_parts.append(rows.astype(BF16))
            right_parts.append(share[q])
        return jnp.dot(
            jnp.concatenate(left_parts, axis=1),
            jnp.concatenate(right_parts, axis=0),
            preferred_element_type=F32,
        ).astype(BF16)

    def send_blocks(t, carry):
        last = ngy - 1 - UNROLL * t
        steps = [last - u for u in range(UNROLL)]
        for i, blocks in zip(steps, [contribution(i) for i in steps]):
            f_send[i] = blocks
            f_copy(i).start()
        return carry

    lax.fori_loop(0, ngy // UNROLL - 1, send_blocks, 0)
    nearest = [contribution(i) for i in range(UNROLL)]
    for i in reversed(range(1, UNROLL)):
        f_send[i] = nearest[i]
        f_copy(i).start()
    f_recv[0] = nearest[0]

    pltpu.make_async_remote_copy(
        src_ref=id_send.at[1:ngy],
        dst_ref=id_recv.at[1:ngy],
        send_sem=id_ss,
        recv_sem=id_rs,
        device_id=(gx, gy),
        device_id_type=MESH,
    ).wait_recv()
    line_of_row = iota((ro, LANES), 0) + 1
    level_of_lane = lax.rem(lax.div(iota((ro, LANES), 1), CAP), GROUP)
    for c in range(chunks):
        ids_row = id_recv[c * CHUNK]
        for t in range(1, CHUNK):
            ids_row = ids_row + id_recv[c * CHUNK + t]
        hit = jnp.where(jnp.broadcast_to(ids_row.astype(I32), (ro, LANES)) == line_of_row, 1.0, 0.0)
        hits[:, c * LANES : (c + 1) * LANES] = hit.astype(BF16)
        for l in range(GROUP):
            spread[c, l * ro : (l + 1) * ro, :] = jnp.where(level_of_lane == l, hit, 0.0).astype(BF16)
    chosen = iota((slots, ngy * SPAN), 0)
    chosen = jnp.where(
        iota((slots, ngy * SPAN), 1) == lax.div(chosen, CAP) * SPAN + lax.rem(chosen, CAP), 1.0, 0.0
    ).astype(BF16)
    pick[...] = lax.dot_general(chosen, hits[...], NT, preferred_element_type=F32).astype(BF16)

    loads[7].wait()

    def land(c, l0, l1):
        base = GROUP * (l0 // GROUP)
        rows = f_recv[c * CHUNK : (c + 1) * CHUNK, base * CAP : base * CAP + SPAN, :]
        landed = jnp.dot(
            spread[c, (l0 - base) * ro : (l1 - base) * ro, :],
            rows.reshape(LANES, LANES),
            preferred_element_type=F32,
        )
        for l in range(l0, l1):
            ocean[l] = ocean[l] + landed[(l - l0) * ro : (l - l0 + 1) * ro]

    for c in reversed(range(chunks)):
        first = 1 if c == 0 else c * CHUNK
        here = pl.ds(first, (c + 1) * CHUNK - first)
        pltpu.make_async_remote_copy(
            src_ref=f_send.at[here],
            dst_ref=f_recv.at[here],
            send_sem=f_ss,
            recv_sem=f_rs.at[c],
            device_id=(gx, gy),
            device_id_type=MESH,
        ).wait_recv()
        if c:
            for l0 in range(0, lo, GROUP):
                land(c, l0, l0 + GROUP)
    land(0, 0, 1)
    top_halo.start(ocean.at[0:1], lambda: pack_sides([ocean[0]], ro))
    land(0, 1, GROUP)
    for l0 in range(GROUP, lo, GROUP):
        land(0, l0, l0 + GROUP)
    low_halo.start(ocean.at[1:lo], lambda: pack_sides([ocean[l] for l in range(1, lo)], ro))

    top_halo.arrive()
    rims[1] = top_halo.rim
    mids[1] = top_halo.mid
    skin = top_halo.two_steps(0, ocean[0], rims.at[1], mids.at[1])
    final[0] = skin
    lines = jnp.dot(pick[...], skin.astype(BF16), preferred_element_type=F32)
    s_send[...] = lines.reshape(ngy, CAP, LANES)
    s_recv[0] = s_send[0]

    def s_copy(i):
        return pltpu.make_async_remote_copy(
            src_ref=s_send.at[i],
            dst_ref=s_recv.at[i],
            send_sem=s_ss,
            recv_sem=s_rs,
            device_id=(gx, behind(i)),
            device_id_type=MESH,
        )

    to_all(lambda i: s_copy(i).start())

    low_halo.arrive()
    rims[2] = low_halo.rim
    mids[2] = low_halo.mid

    for n in range(lo - 1):
        final[n + 1] = low_halo.two_steps(n, ocean[n + 1], rims.at[2], mids.at[2])
    final_copy = pltpu.make_async_copy(final, final_hbm, final_sem)
    final_copy.start()

    rest = pl.ds(1, ngy - 1)
    pltpu.make_async_remote_copy(
        src_ref=s_send.at[rest],
        dst_ref=s_recv.at[rest],
        send_sem=s_ss,
        recv_sem=s_rs,
        device_id=(gx, gy),
        device_id_type=MESH,
    ).wait_recv()
    home_lines[...] = s_recv[...].reshape(slots, 1, LANES)
    row_a = iota((ra, LANES), 0)

    def home(b, total):
        return sum([part(b * UNROLL + u) for u in range(UNROLL)], total)

    def part(b):
        left_parts, right_parts = [], []
        for j in range(4):
            q = b * 4 + j
            line = jnp.broadcast_to(home_lines[jnp.clip(table_s[0, q], 0, slots - 1)], (ra, LANES))
            left_parts.append(jnp.where(row_a == src_ref[0, q], line, 0.0).astype(BF16))
            right_parts.append(share[q])
        return lax.dot_general(
            jnp.concatenate(left_parts, axis=1),
            jnp.concatenate(right_parts, axis=1),
            NT,
            preferred_element_type=F32,
        )

    aerial_ref[...] = lax.fori_loop(0, nb // (4 * UNROLL), home, jnp.zeros((ra, LANES), F32))

    for halo in (atm_halo, top_halo, low_halo):
        halo.wait_sent()
    for buffer, sem, first in ((id_send, id_ss, 1), (f_send, f_ss, 1), (s_send, s_ss, 1)):
        here = pl.ds(first, buffer.shape[0] - first)
        pltpu.make_async_remote_copy(
            src_ref=buffer.at[here],
            dst_ref=buffer.at[here],
            send_sem=sem,
            recv_sem=s_rs,
            device_id=(gx, gy),
            device_id_type=MESH,
        ).wait_send()
    final_copy.wait()


def halo_scratch(rows, count):
    cs = -(-2 * count // 8) * 8
    return [
        pltpu.VMEM((count, 8, LANES), F32),
        pltpu.VMEM((count, 8, LANES), F32),
        pltpu.VMEM((cs, LANES), F32),
        pltpu.VMEM((cs, LANES), F32),
        pltpu.VMEM((4, 8, LANES), F32),
        pltpu.VMEM((cs, LANES), F32),
        pltpu.VMEM((cs, LANES), F32),
        pltpu.VMEM((2, 8, LANES), F32),
        pltpu.VMEM((rows, LANES), F32),
        pltpu.SemaphoreType.DMA((8,)),
        pltpu.SemaphoreType.DMA((8,)),
    ]


def body(sizes, atm_state, ocean_temp, flux_coef, flux_mix, share, src, dest, owner):
    ngx, nx, nz = sizes
    ngy = nx * nz
    slots = ngy * CAP
    la, ra, _ = atm_state.shape
    lo, ro, _ = ocean_temp.shape
    nb = src.shape[1]
    vmem = pl.BlockSpec(memory_space=pltpu.VMEM)
    far = pl.BlockSpec(memory_space=pltpu.HBM)
    dma = pltpu.SemaphoreType.DMA
    return pl.pallas_call(
        functools.partial(kernel, sizes),
        out_shape=(
            jax.ShapeDtypeStruct(ocean_temp.shape, F32),
            jax.ShapeDtypeStruct((ra, LANES), F32),
        ),
        in_specs=[far] * 8,
        out_specs=(far, vmem),
        scratch_shapes=[
            pltpu.VMEM(atm_state.shape, F32),
            pltpu.SMEM(flux_coef.shape[::-1], F32),
            pltpu.SMEM(flux_mix.shape, F32),
            pltpu.SMEM((1, nb), I32),
            pltpu.VMEM((1, nb), I32),
            pltpu.VMEM((1, nb), I32),
            pltpu.VMEM((nb, LANES, LANES), BF16),
            pltpu.VMEM((lo, ro, LANES), F32),
            pltpu.VMEM((lo, ro, LANES), F32),
            pltpu.VMEM((la, ra, LANES), F32),
            pltpu.VMEM((lo * CAP * ra, LANES), F32),
            pltpu.VMEM((8, LANES), I32),
            pltpu.VMEM((8, LANES), I32),
            pltpu.SMEM((8, LANES), I32),
            pltpu.VMEM((ngy, 1, LANES), F32),
            pltpu.VMEM((ngy, 1, LANES), F32),
            pltpu.VMEM((ngy, lo * CAP, LANES), BF16),
            pltpu.VMEM((ngy, lo * CAP, LANES), BF16),
            pltpu.VMEM((ro, ngy * SPAN), BF16),
            pltpu.VMEM((ngy // CHUNK, GROUP * ro, LANES), BF16),
            pltpu.VMEM((slots, ro), BF16),
            pltpu.VMEM((ngy, CAP, LANES), F32),
            pltpu.VMEM((ngy, CAP, LANES), F32),
            pltpu.VMEM((slots, 1, LANES), F32),
            pltpu.VMEM((3, ro + 16, LANES), F32),
            pltpu.VMEM((3, ro, LANES), F32),
            dma((8,)),
            dma,
            dma,
            dma,
            dma,
            dma,
            dma((ngy // CHUNK,)),
            dma,
            dma,
            *halo_scratch(ra, la),
            *halo_scratch(ro, 1),
            *halo_scratch(ro, lo - 1),
        ],
        compiler_params=pltpu.CompilerParams(
            collective_id=0, has_side_effects=True, vmem_limit_bytes=48 * 1024 * 1024
        ),
        cost_estimate=pl.CostEstimate(flops=200_000_000, bytes_accessed=5_000_000, transcendentals=100_000),
    )(
        *(
            pltpu.with_memory_space_constraint(x, pltpu.HBM)
            for x in (atm_state, ocean_temp, flux_coef.T, flux_mix, share, src, dest, owner.reshape(1, nb))
        )
    )


def solution(mesh):
    ngy = mesh.shape["gy"]
    nx = 4
    return jax.shard_map(
        functools.partial(body, (mesh.shape["gx"], nx, ngy // nx)),
        mesh=mesh,
        in_specs=(
            P(None, "gx", "gy"),
            P(None, "gx", "gy"),
            P(),
            P(),
            P("gx", "gy", None, None),
            P("gx", "gy"),
            P("gx", "gy"),
            P("gx", "gy", None),
        ),
        out_specs=(P(None, "gx", "gy"), P("gx", "gy")),
        check_vma=False,
    )
```

```python
import functools

import jax
import jax.numpy as jnp
from jax import lax
from jax.experimental import pallas as pl
from jax.experimental.pallas import tpu as pltpu
from jax.sharding import PartitionSpec as P

MESH = pl.DeviceIdType.MESH
RATE = 0.2
CAP = 4
F32, BF16, I32 = jnp.float32, jnp.bfloat16, jnp.int32
LANES = 128
NT = (((1,), (1,)), ((), ()))
GROUP = 2
SPAN = GROUP * CAP
CHUNK = LANES // SPAN
UNROLL = 4
BURST = 8


def iota(shape, dim):
    return lax.broadcasted_iota(I32, shape, dim)


def pack_sides(levels, rows):
    pair = lax.shift_right_logical(iota((rows, LANES), 1), 1)
    packed = jnp.zeros((rows, LANES), F32)
    for n, field in enumerate(levels):
        packed = jnp.where(pair == n, pltpu.roll(field, 2 * n, 1) if n else field, packed)
        packed = jnp.where(pair == 32 + n, pltpu.roll(field, 66 + 2 * n, 1), packed)
    return packed


class Halo:
    def __init__(self, place, refs, rows, count):
        self.gx, self.gy, self.ngx, self.ngy = place
        (self.top, self.bot, self.cl, self.cr, self.dg, self.ptl, self.ptr, self.pe, self.pk, self.ss, self.rs) = refs
        self.rows, self.count = rows, count

    def start(self, field, levels):
        rows = self.rows
        up, down = lax.rem(self.gx + self.ngx - 1, self.ngx), lax.rem(self.gx + 1, self.ngx)
        left, right = lax.rem(self.gy + self.ngy - 1, self.ngy), lax.rem(self.gy + 1, self.ngy)
        plan = (
            (field.at[:, 0:8], self.bot, (up, self.gy)),
            (field.at[:, rows - 8 : rows], self.top, (down, self.gy)),
            (self.ptl, self.cr, (self.gx, left)),
            (self.ptr, self.cl, (self.gx, right)),
            (self.pe.at[0], self.dg.at[3], (up, left)),
            (self.pe.at[0], self.dg.at[2], (up, right)),
            (self.pe.at[1], self.dg.at[1], (down, left)),
            (self.pe.at[1], self.dg.at[0], (down, right)),
        )
        self.copies = [
            pltpu.make_async_remote_copy(
                src_ref=src,
                dst_ref=dst,
                send_sem=self.ss.at[n],
                recv_sem=self.rs.at[n],
                device_id=device,
                device_id_type=MESH,
            )
            for n, (src, dst, device) in enumerate(plan)
        ]
        for copy in self.copies[0:2]:
            copy.start()
        packed = levels() if callable(levels) else levels
        self.pe[0] = packed[0:8]
        self.pe[1] = packed[rows - 8 : rows]
        for copy in self.copies[4:8]:
            copy.start()
        tall = packed
        if rows < LANES:
            tall = jnp.concatenate([packed, jnp.zeros((LANES - rows, LANES), F32)], axis=0)
        turned = tall.T
        cs = self.ptl.shape[0]
        self.ptl[...] = turned[0:cs]
        self.ptr[...] = turned[64 : 64 + cs]
        self.pk[...] = packed
        for copy in self.copies[2:4]:
            copy.start()

    def arrive(self):
        for copy in self.copies:
            copy.wait_recv()
        rows = self.rows
        lane = iota((1, LANES), 1)
        low = lane < 64
        self.has_top, self.has_bot = self.gx > 0, self.gx < self.ngx - 1
        edge = jnp.where(low, jnp.where(self.gy > 0, 1, 0), jnp.where(self.gy < self.ngy - 1, 1, 0)) > 0
        cs = self.cl.shape[0]
        fill = jnp.zeros((64 - cs, LANES), F32)
        turned = jnp.concatenate([self.cl[...], fill, self.cr[...], fill], axis=0)
        sides = turned.T[0:rows]
        above = jnp.where(low, pltpu.roll(self.dg[0], 64, 1), pltpu.roll(self.dg[1], 64, 1))
        below = jnp.where(low, pltpu.roll(self.dg[2], 64, 1), pltpu.roll(self.dg[3], 64, 1))
        above = jnp.where(self.has_top, above, 0.0)
        below = jnp.where(self.has_bot, below, 0.0)
        rim = jnp.where(edge, jnp.concatenate([above, sides, below], axis=0), 0.0)
        total = rows + 16
        up = pltpu.roll(rim, 1, 0)[8 : rows + 8]
        down = pltpu.roll(rim, total - 1, 0)[8 : rows + 8]
        near = sides + self.pk[...]
        beside = jnp.where(low, pltpu.roll(near, 1, 1), pltpu.roll(near, LANES - 1, 1))
        mid = sides + RATE * (up + down + beside - 4.0 * sides)
        mid = jnp.where(edge, mid, 0.0)
        odd = lax.rem(lane, 2) == 1
        self.rim = jnp.where(odd, rim, pltpu.roll(rim, 64, 1))
        self.mid = jnp.where(odd, mid, pltpu.roll(mid, 64, 1))

    def two_steps(self, n, field, rim_ref, mid_ref):
        rows = self.rows
        total = rows + 16
        rim, rim_mid = rim_ref[...], mid_ref[...]
        top = jnp.where(self.has_top, self.top[n], 0.0)
        bot = jnp.where(self.has_bot, self.bot[n], 0.0)
        whole = jnp.concatenate([top, field, bot], axis=0)
        lane, row = iota((total, LANES), 1), iota((total, LANES), 0)
        to_ends = LANES - 1 - 2 * n
        side = pltpu.roll(rim, to_ends, 1)
        beside = (
            jnp.where(lane == 0, side, pltpu.roll(whole, 1, 1))
            + jnp.where(lane == LANES - 1, side, pltpu.roll(whole, LANES - 1, 1))
            + pltpu.roll(whole, 1, 0)
            + pltpu.roll(whole, total - 1, 0)
        )
        mid = whole + RATE * (beside - 4.0 * whole)
        first_row, last_row = jnp.where(self.has_top, 0, 8), jnp.where(self.has_bot, total, rows + 8)
        mid = jnp.where((row >= first_row) & (row < last_row), mid, 0.0)
        own = mid[8 : rows + 8]
        lane = iota((rows, LANES), 1)
        side = pltpu.roll(rim_mid, to_ends, 1)
        beside = (
            jnp.where(lane == 0, side, pltpu.roll(own, 1, 1))
            + jnp.where(lane == LANES - 1, side, pltpu.roll(own, LANES - 1, 1))
            + pltpu.roll(mid, 1, 0)[8 : rows + 8]
            + pltpu.roll(mid, total - 1, 0)[8 : rows + 8]
        )
        return own + RATE * (beside - 4.0 * own)

    def wait_sent(self):
        for copy in self.copies:
            copy.wait_send()


def kernel(
    sizes,
    atm_hbm,
    ocean_hbm,
    coef_hbm,
    mix_hbm,
    share_hbm,
    src_hbm,
    dest_hbm,
    owner_hbm,
    final_hbm,
    aerial_ref,
    atm_ref,
    coef_ref,
    mix_ref,
    src_ref,
    dest_ref,
    owner_ref,
    share,
    ocean,
    final,
    surf,
    mixed,
    lists,
    table,
    table_s,
    id_send,
    id_recv,
    f_send,
    f_recv,
    hits,
    spread,
    pick,
    s_send,
    s_recv,
    home_lines,
    rims,
    mids,
    in_sems,
    table_sem,
    final_sem,
    id_ss,
    id_rs,
    f_ss,
    f_rs,
    s_ss,
    s_rs,
    *halo_refs,
):
    ngx, nx, nz = sizes
    ngy = nx * nz
    slots = ngy * CAP
    chunks = ngy // CHUNK
    la, ra = atm_ref.shape[0], atm_ref.shape[1]
    lo, ro = ocean.shape[0], ocean.shape[1]
    nb = src_ref.shape[1]
    fluxes = coef_ref.shape[1]
    gx, gy = lax.axis_index("gx"), lax.axis_index("gy")
    my_x, my_z = lax.div(gy, nz), lax.rem(gy, nz)
    place = (gx, gy, ngx, ngy)

    loads = [
        pltpu.make_async_copy(far, near, in_sems.at[n])
        for n, (far, near) in enumerate(
            (
                (owner_hbm, owner_ref),
                (dest_hbm, dest_ref),
                (atm_hbm, atm_ref),
                (coef_hbm, coef_ref),
                (mix_hbm, mix_ref),
                (src_hbm, src_ref),
                (share_hbm.at[0], share),
                (ocean_hbm, ocean),
            )
        )
    ]
    for load in loads:
        load.start()

    def shift(i):
        k = lax.div(i, nx)
        dx = lax.rem(i, nx)
        dz = lax.div(k + 1, 2) * (2 * lax.rem(k, 2) - 1)
        return dx, dz

    def ahead(i):
        dx, dz = shift(i)
        return lax.rem(my_x + dx, nx) * nz + lax.rem(my_z + dz + nz, nz)

    def behind(i):
        dx, dz = shift(i)
        return lax.rem(my_x - dx + nx, nx) * nz + lax.rem(my_z - dz + nz, nz)

    def to_all(act):
        def burst(t, carry):
            for u in range(BURST):
                act(ngy - 1 - BURST * t - u)
            return carry

        lax.fori_loop(0, ngy // BURST - 1, burst, 0)
        for i in reversed(range(1, BURST)):
            act(i)

    barrier = pltpu.get_barrier_semaphore()
    up, down = lax.rem(gx + ngx - 1, ngx), lax.rem(gx + 1, ngx)
    left, right = lax.rem(gy + ngy - 1, ngy), lax.rem(gy + 1, ngy)
    for device in ((up, gy), (down, gy), (up, left), (up, right), (down, left), (down, right)):
        pl.semaphore_signal(barrier, inc=1, device_id=device, device_id_type=MESH)

    to_all(lambda i: pl.semaphore_signal(barrier, inc=1, device_id=(gx, ahead(i)), device_id_type=MESH))

    atm_halo = Halo(place, halo_refs[0:11], ra, la)
    top_halo = Halo(place, halo_refs[11:22], ro, 1)
    low_halo = Halo(place, halo_refs[22:33], ro, lo - 1)

    for load in loads[0:3]:
        load.wait()
    lists[...] = jnp.full((8, LANES), -1, I32)
    lists[0:1, 0:nb] = owner_ref[...]
    lists[1:2, 0:nb] = dest_ref[...]
    own_row, dest_row = lists[0:1, :], lists[1:2, :]
    lane = iota((1, LANES), 1)
    own_x = jnp.zeros((1, LANES), I32)
    for t in range(1, nx):
        own_x = own_x + jnp.where(own_row >= t * nz, 1, 0)
    own_z = own_row - own_x * nz
    dx = own_x - my_x
    dx = jnp.where(dx < 0, dx + nx, dx)
    dz = own_z - my_z
    dz = jnp.where(dz < 0, dz + nz, dz)
    k = jnp.where(dz == 0, 0, jnp.where(dz <= nz // 2, 2 * dz - 1, 2 * (nz - dz)))
    step_row = k * nx + dx
    sq = (LANES, LANES)
    sub_q, lane_q = iota(sq, 0), iota(sq, 1)
    own_sq = jnp.broadcast_to(own_row, sq)
    same = (own_sq == own_sq.T) & (sub_q < lane_q)
    rank = jnp.sum(jnp.where(same, 1, 0), axis=0, keepdims=True)
    slot_row = jnp.where(lane < nb, step_row * CAP + rank, -1)
    slot_col = jnp.broadcast_to(slot_row, sq).T
    table[...] = jnp.zeros((8, LANES), I32)
    table[0:1, :] = jnp.clip(slot_row, 0, slots - 1)
    for b in range(-(-slots // LANES)):
        hit = slot_col == lane_q + b * LANES
        block = jnp.sum(jnp.where(hit, sub_q, 0), axis=0, keepdims=True)
        table[1 + b : 2 + b, :] = jnp.clip(block, 0, nb - 1)
    table_copy = pltpu.make_async_copy(table, table_s, table_sem)
    table_copy.start()
    wide = (ngy, LANES)
    step_i, lane_i = iota(wide, 0), iota(wide, 1)
    slot_w = jnp.broadcast_to(slot_row, wide)
    line_w = jnp.broadcast_to((dest_row + 1).astype(F32), wide)
    ids = jnp.zeros(wide, F32)
    for j in range(CAP):
        line = jnp.sum(jnp.where(slot_w == step_i * CAP + j, line_w, 0.0), axis=1, keepdims=True)
        ids = jnp.where(lax.rem(lane_i, CAP) == j, jnp.broadcast_to(line, wide), ids)
    ids = jnp.where(lax.div(lane_i, SPAN) == lax.rem(step_i, CHUNK), ids, 0.0)
    id_send[...] = ids.reshape(ngy, 1, LANES)
    id_recv[0] = id_send[0]

    atm_packed = pack_sides([atm_ref[l] for l in range(la)], ra)

    pl.semaphore_wait(barrier, ngy - 1 + 6)

    atm_halo.start(atm_ref, atm_packed)

    def id_copy(i):
        return pltpu.make_async_remote_copy(
            src_ref=id_send.at[i],
            dst_ref=id_recv.at[i],
            send_sem=id_ss,
            recv_sem=id_rs,
            device_id=(gx, ahead(i)),
            device_id_type=MESH,
        )

    to_all(lambda i: id_copy(i).start())

    atm_halo.arrive()
    rims[0, 0 : ra + 16] = atm_halo.rim
    mids[0, 0:ra] = atm_halo.mid

    for l in range(la):
        surf[l] = atm_halo.two_steps(l, atm_ref[l], rims.at[0, 0 : ra + 16], mids.at[0, 0:ra])

    for load in loads[3:5]:
        load.wait()

    band = 16

    def flux_band(c, carry):
        r0 = pl.multiple_of(c * band, band)
        fields = [surf[l, pl.ds(r0, band)] for l in range(la)]
        flux = []
        for kk in range(fluxes):
            total = coef_ref[0, kk] * fields[0]
            for l in range(1, la):
                total = total + coef_ref[l, kk] * fields[l]
            flux.append(jnp.tanh(total).astype(BF16).astype(F32))
        for l in range(lo):
            total = mix_ref[l, 0] * flux[0]
            for kk in range(1, fluxes):
                total = total + mix_ref[l, kk] * flux[kk]
            total = 0.5 * total
            for j in range(CAP):
                mixed[pl.ds(pl.multiple_of((l * CAP + j) * ra + r0, band), band)] = total
        return carry

    lax.fori_loop(0, ra // band, flux_band, 0)

    table_copy.wait()
    for load in loads[5:7]:
        load.wait()

    used = lo * CAP
    slot_of_row = lax.rem(iota((used, LANES), 0), CAP)

    def f_copy(i):
        return pltpu.make_async_remote_copy(
            src_ref=f_send.at[i],
            dst_ref=f_recv.at[i],
            send_sem=f_ss,
            recv_sem=f_rs.at[lax.div(i, CHUNK)],
            device_id=(gx, ahead(i)),
            device_id_type=MESH,
        )

    def contribution(i):
        left_parts, right_parts = [], []
        for j in range(CAP):
            s = i * CAP + j
            q = jnp.clip(table_s[1 + lax.div(s, LANES), lax.rem(s, LANES)], 0, nb - 1)
            rows = mixed[pl.ds(src_ref[0, q], used, stride=ra), :]
            rows = jnp.where(slot_of_row == j, rows, 0.0)
            left_parts.append(rows.astype(BF16))
            right_parts.append(share[q])
        return jnp.dot(
            jnp.concatenate(left_parts, axis=1),
            jnp.concatenate(right_parts, axis=0),
            preferred_element_type=F32,
        ).astype(BF16)

    def send_blocks(t, carry):
        last = ngy - 1 - UNROLL * t
        steps = [last - u for u in range(UNROLL)]
        for i, blocks in zip(steps, [contribution(i) for i in steps]):
            f_send[i] = blocks
            f_copy(i).start()
        return carry

    lax.fori_loop(0, ngy // UNROLL - 1, send_blocks, 0)
    nearest = [contribution(i) for i in range(UNROLL)]
    for i in reversed(range(1, UNROLL)):
        f_send[i] = nearest[i]
        f_copy(i).start()
    f_recv[0] = nearest[0]

    pltpu.make_async_remote_copy(
        src_ref=id_send.at[1:ngy],
        dst_ref=id_recv.at[1:ngy],
        send_sem=id_ss,
        recv_sem=id_rs,
        device_id=(gx, gy),
        device_id_type=MESH,
    ).wait_recv()
    line_of_row = iota((ro, LANES), 0) + 1
    level_of_lane = lax.rem(lax.div(iota((ro, LANES), 1), CAP), GROUP)
    for c in range(chunks):
        ids_row = id_recv[c * CHUNK]
        for t in range(1, CHUNK):
            ids_row = ids_row + id_recv[c * CHUNK + t]
        hit = jnp.where(jnp.broadcast_to(ids_row.astype(I32), (ro, LANES)) == line_of_row, 1.0, 0.0)
        hits[:, c * LANES : (c + 1) * LANES] = hit.astype(BF16)
        for l in range(GROUP):
            spread[c, l * ro : (l + 1) * ro, :] = jnp.where(level_of_lane == l, hit, 0.0).astype(BF16)
    chosen = iota((slots, ngy * SPAN), 0)
    chosen = jnp.where(
        iota((slots, ngy * SPAN), 1) == lax.div(chosen, CAP) * SPAN + lax.rem(chosen, CAP), 1.0, 0.0
    ).astype(BF16)
    pick[...] = lax.dot_general(chosen, hits[...], NT, preferred_element_type=F32).astype(BF16)

    loads[7].wait()

    def land(c, l0, l1):
        base = GROUP * (l0 // GROUP)
        rows = f_recv[c * CHUNK : (c + 1) * CHUNK, base * CAP : base * CAP + SPAN, :]
        landed = jnp.dot(
            spread[c, (l0 - base) * ro : (l1 - base) * ro, :],
            rows.reshape(LANES, LANES),
            preferred_element_type=F32,
        )
        for l in range(l0, l1):
            ocean[l] = ocean[l] + landed[(l - l0) * ro : (l - l0 + 1) * ro]

    for c in reversed(range(chunks)):
        first = 1 if c == 0 else c * CHUNK
        here = pl.ds(first, (c + 1) * CHUNK - first)
        pltpu.make_async_remote_copy(
            src_ref=f_send.at[here],
            dst_ref=f_recv.at[here],
            send_sem=f_ss,
            recv_sem=f_rs.at[c],
            device_id=(gx, gy),
            device_id_type=MESH,
        ).wait_recv()
        if c:
            for l0 in range(0, lo, GROUP):
                land(c, l0, l0 + GROUP)
    land(0, 0, 1)
    top_halo.start(ocean.at[0:1], lambda: pack_sides([ocean[0]], ro))
    land(0, 1, GROUP)
    for l0 in range(GROUP, lo, GROUP):
        land(0, l0, l0 + GROUP)
    low_halo.start(ocean.at[1:lo], lambda: pack_sides([ocean[l] for l in range(1, lo)], ro))

    top_halo.arrive()
    rims[1] = top_halo.rim
    mids[1] = top_halo.mid
    skin = top_halo.two_steps(0, ocean[0], rims.at[1], mids.at[1])
    final[0] = skin
    lines = jnp.dot(pick[...], skin.astype(BF16), preferred_element_type=F32)
    s_send[...] = lines.astype(BF16).reshape(ngy, CAP, LANES)
    s_recv[0] = s_send[0]

    def s_copy(i):
        return pltpu.make_async_remote_copy(
            src_ref=s_send.at[i],
            dst_ref=s_recv.at[i],
            send_sem=s_ss,
            recv_sem=s_rs,
            device_id=(gx, behind(i)),
            device_id_type=MESH,
        )

    to_all(lambda i: s_copy(i).start())

    low_halo.arrive()
    rims[2] = low_halo.rim
    mids[2] = low_halo.mid

    for n in range(lo - 1):
        final[n + 1] = low_halo.two_steps(n, ocean[n + 1], rims.at[2], mids.at[2])
    final_copy = pltpu.make_async_copy(final, final_hbm, final_sem)
    final_copy.start()

    rest = pl.ds(1, ngy - 1)
    pltpu.make_async_remote_copy(
        src_ref=s_send.at[rest],
        dst_ref=s_recv.at[rest],
        send_sem=s_ss,
        recv_sem=s_rs,
        device_id=(gx, gy),
        device_id_type=MESH,
    ).wait_recv()
    home_lines[...] = s_recv[...].astype(F32).reshape(slots, 1, LANES)
    row_a = iota((ra, LANES), 0)

    def home(b, total):
        return sum([part(b * UNROLL + u) for u in range(UNROLL)], total)

    def part(b):
        left_parts, right_parts = [], []
        for j in range(4):
            q = b * 4 + j
            line = jnp.broadcast_to(home_lines[jnp.clip(table_s[0, q], 0, slots - 1)], (ra, LANES))
            left_parts.append(jnp.where(row_a == src_ref[0, q], line, 0.0).astype(BF16))
            right_parts.append(share[q])
        return lax.dot_general(
            jnp.concatenate(left_parts, axis=1),
            jnp.concatenate(right_parts, axis=1),
            NT,
            preferred_element_type=F32,
        )

    aerial_ref[...] = lax.fori_loop(0, nb // (4 * UNROLL), home, jnp.zeros((ra, LANES), F32))

    for halo in (atm_halo, top_halo, low_halo):
        halo.wait_sent()
    for buffer, sem, first in ((id_send, id_ss, 1), (f_send, f_ss, 1), (s_send, s_ss, 1)):
        here = pl.ds(first, buffer.shape[0] - first)
        pltpu.make_async_remote_copy(
            src_ref=buffer.at[here],
            dst_ref=buffer.at[here],
            send_sem=sem,
            recv_sem=s_rs,
            device_id=(gx, gy),
            device_id_type=MESH,
        ).wait_send()
    final_copy.wait()


def halo_scratch(rows, count):
    cs = -(-2 * count // 8) * 8
    return [
        pltpu.VMEM((count, 8, LANES), F32),
        pltpu.VMEM((count, 8, LANES), F32),
        pltpu.VMEM((cs, LANES), F32),
        pltpu.VMEM((cs, LANES), F32),
        pltpu.VMEM((4, 8, LANES), F32),
        pltpu.VMEM((cs, LANES), F32),
        pltpu.VMEM((cs, LANES), F32),
        pltpu.VMEM((2, 8, LANES), F32),
        pltpu.VMEM((rows, LANES), F32),
        pltpu.SemaphoreType.DMA((8,)),
        pltpu.SemaphoreType.DMA((8,)),
    ]


def body(sizes, atm_state, ocean_temp, flux_coef, flux_mix, share, src, dest, owner):
    ngx, nx, nz = sizes
    ngy = nx * nz
    slots = ngy * CAP
    la, ra, _ = atm_state.shape
    lo, ro, _ = ocean_temp.shape
    nb = src.shape[1]
    vmem = pl.BlockSpec(memory_space=pltpu.VMEM)
    far = pl.BlockSpec(memory_space=pltpu.HBM)
    dma = pltpu.SemaphoreType.DMA
    return pl.pallas_call(
        functools.partial(kernel, sizes),
        out_shape=(
            jax.ShapeDtypeStruct(ocean_temp.shape, F32),
            jax.ShapeDtypeStruct((ra, LANES), F32),
        ),
        in_specs=[far] * 8,
        out_specs=(far, vmem),
        scratch_shapes=[
            pltpu.VMEM(atm_state.shape, F32),
            pltpu.SMEM(flux_coef.shape[::-1], F32),
            pltpu.SMEM(flux_mix.shape, F32),
            pltpu.SMEM((1, nb), I32),
            pltpu.VMEM((1, nb), I32),
            pltpu.VMEM((1, nb), I32),
            pltpu.VMEM((nb, LANES, LANES), BF16),
            pltpu.VMEM((lo, ro, LANES), F32),
            pltpu.VMEM((lo, ro, LANES), F32),
            pltpu.VMEM((la, ra, LANES), F32),
            pltpu.VMEM((lo * CAP * ra, LANES), F32),
            pltpu.VMEM((8, LANES), I32),
            pltpu.VMEM((8, LANES), I32),
            pltpu.SMEM((8, LANES), I32),
            pltpu.VMEM((ngy, 1, LANES), F32),
            pltpu.VMEM((ngy, 1, LANES), F32),
            pltpu.VMEM((ngy, lo * CAP, LANES), BF16),
            pltpu.VMEM((ngy, lo * CAP, LANES), BF16),
            pltpu.VMEM((ro, ngy * SPAN), BF16),
            pltpu.VMEM((ngy // CHUNK, GROUP * ro, LANES), BF16),
            pltpu.VMEM((slots, ro), BF16),
            pltpu.VMEM((ngy, CAP, LANES), BF16),
            pltpu.VMEM((ngy, CAP, LANES), BF16),
            pltpu.VMEM((slots, 1, LANES), F32),
            pltpu.VMEM((3, ro + 16, LANES), F32),
            pltpu.VMEM((3, ro, LANES), F32),
            dma((8,)),
            dma,
            dma,
            dma,
            dma,
            dma,
            dma((ngy // CHUNK,)),
            dma,
            dma,
            *halo_scratch(ra, la),
            *halo_scratch(ro, 1),
            *halo_scratch(ro, lo - 1),
        ],
        compiler_params=pltpu.CompilerParams(
            collective_id=0, has_side_effects=True, vmem_limit_bytes=48 * 1024 * 1024
        ),
        cost_estimate=pl.CostEstimate(flops=200_000_000, bytes_accessed=5_000_000, transcendentals=100_000),
    )(
        *(
            pltpu.with_memory_space_constraint(x, pltpu.HBM)
            for x in (atm_state, ocean_temp, flux_coef.T, flux_mix, share, src, dest, owner.reshape(1, nb))
        )
    )


def solution(mesh):
    ngy = mesh.shape["gy"]
    nx = 4
    return jax.shard_map(
        functools.partial(body, (mesh.shape["gx"], nx, ngy // nx)),
        mesh=mesh,
        in_specs=(
            P(None, "gx", "gy"),
            P(None, "gx", "gy"),
            P(),
            P(),
            P("gx", "gy", None, None),
            P("gx", "gy"),
            P("gx", "gy"),
            P("gx", "gy", None),
        ),
        out_specs=(P(None, "gx", "gy"), P("gx", "gy")),
        check_vma=False,
    )
```
